256 devices in a mesh: sub: 32 (over z, x), lvl: 8 (over y, core).
Axes of the slice: x: 4, y: 4, z: 8, core: 2. Of those that a mesh axis runs over, the one named last changes fastest.
Arguments:
- rhs: bfloat16 [8, 1024, 256, 128], P('lvl', 'sub'), may hold values from -6 to 6
- inverse_blocks: bfloat16 [8, 1024, 256, 256], P('lvl', 'sub'), as said below
- update_blocks: bfloat16 [8, 1024, 32, 256], P('lvl', 'sub'), may hold values from -0.75 to 0.75
- parent_owner: int32 [8, 1024, 1], replicated, may hold values from 0 to 31; in each aligned block of 32 rows (0 to 31, 32 to 63, ..., all dimensions but the last counted through in order) at most 2 rows name the same one
- parent_slot: int32 [8, 1024], replicated, may hold values from 0 to 31
- update_rows: int32 [8, 1024, 32], replicated, may hold values from 0 to 255, as said below
Outputs:
- solution: bfloat16 [8, 1024, 256, 128], P('lvl', 'sub')
The draws below stay inside these ranges and needn't reach their ends.
Inputs may be any that keep to these rules, and one draw needn't show every extreme that they name: `parent_owner`: within each tree level, the 32 supernodes n = s * 32 to (s + 1) * 32 - 1 name any one index of sub at most 2 times; in some levels and for some s an index is named exactly 2 times. `update_rows`: each list names 32 different columns in rising order. `inverse_blocks`: each block is lower triangular with a diagonal of 0.6 to 1.4.
All inputs are finite; a program needn't handle non-finite values.
Results may differ from the reference program's by a relative error of at most 0.012.
Values may be sent and summed in bfloat16 or wider, within the bound.
No kernel may reach another device: no remote copies, remote signals or barrier semaphores. Data moves between devices by JAX's collectives and lax.ppermute only.
A program may use at most 64 MiB of HBM per device.

```python
import math
import jax
import jax.numpy as jnp
import numpy as np
from jax import lax

W = 256
U = 32
R = 128
SN_DEV = 32
CAP = 2
SUPERNODES = 1024
LEVELS = 8
N_SUB = 32


def draw_inverse_blocks(key, part):
    key = jax.random.fold_in(key, 11)
    key_one, key_two = jax.random.split(key)
    full_shape = (LEVELS, SUPERNODES, W, W)
    spread = jax.random.normal(key_one, full_shape, jnp.float32)
    diagonal = jax.random.uniform(key_two, (LEVELS, SUPERNODES, W), jnp.float32, 0.6, 1.4)
    rows_at = lax.broadcasted_iota(jnp.int32, (W, W), 0)
    cols_at = lax.broadcasted_iota(jnp.int32, (W, W), 1)
    strict_lower = jnp.where(rows_at > cols_at, spread * (0.7 / math.sqrt(W)), 0.0)
    identity = jnp.where(rows_at == cols_at, 1.0, 0.0)
    return (strict_lower + identity * diagonal[..., :, None]).astype(jnp.bfloat16)


def draw_update_rows(key, part):
    key = jax.random.fold_in(key, 23)
    scores = jax.random.randint(key, (LEVELS, SUPERNODES, W), 0, 1 << 20)
    scores = scores * W + lax.broadcasted_iota(jnp.int32, (LEVELS, SUPERNODES, W), 2)
    chosen = lax.top_k(scores, U)[1]
    return jnp.sort(chosen, axis=-1).astype(jnp.int32)


def set_ends(result, stream_key, smallest, largest):
    spot = [jax.random.randint(jax.random.fold_in(stream_key, axis), (), 0, length) for axis, length in enumerate(result.shape)]
    longest = result.shape.index(max(result.shape))
    next_to = spot[:longest] + [(spot[longest] + 1) % result.shape[longest]] + spot[longest + 1:]
    return result.at[tuple(spot)].set(smallest).at[tuple(next_to)].set(largest)


def block_levels(stream_key, shape, shards, low, top_value):
    loudness, own = 1.0, jax.random.fold_in(stream_key, 6)
    for axis_at, blocks in shards:
        heights = jnp.exp(jax.random.uniform(jax.random.fold_in(own, axis_at), (blocks,), jnp.float32, low / len(shards), top_value / len(shards)))
        loudness = loudness * jnp.repeat(heights, shape[axis_at] // blocks).reshape([-1 if axis == axis_at else 1 for axis in range(len(shape))])
    return loudness


def shared_out(key, own, number, rows, count, top, most, slope):
    ranking = jax.random.permutation(key, count)
    packed, common = shares(count, rows * top, most, slope, True), shares(count, rows * top, most, slope, False)
    places = jnp.arange(count)

    def named(lengths, turn):
        used = int((lengths > 0).sum())
        fixed = max(1, used // 4)
        moved = fixed + (places - fixed + turn * (used - fixed)) % max(1, count - fixed)
        return jnp.zeros((count,), jnp.int32).at[ranking[jnp.where(places < fixed, places, moved)]].set(jnp.asarray(lengths, jnp.int32))

    lengths = jnp.where(number % 4 == 0, named(packed, number // 4), named(common, number - number // 4 - 1))
    mixed = jax.random.permutation(jax.random.fold_in(own, 3), count)
    donor, sink = mixed[0:count // 2 * 2:2], mixed[1:count // 2 * 2:2]
    slack = jnp.minimum(lengths[donor] - 1, most - lengths[sink]) // 2
    slack = jnp.where((donor == ranking[0]) | (sink == ranking[0]) | (lengths[sink] == 0), 0, jnp.maximum(slack, 0))
    moved = jax.random.randint(jax.random.fold_in(own, 4), (count // 2,), 0, 1 << 20) % (slack + 1)
    lengths = lengths.at[donor].add(-moved).at[sink].add(moved)
    members = jnp.searchsorted(jnp.cumsum(lengths), jnp.arange(rows * top), side="right").astype(jnp.int32)
    listing = members.reshape(top, rows).T
    listing = listing[jax.random.permutation(jax.random.fold_in(own, 1), rows)]
    turn = jax.random.randint(jax.random.fold_in(own, 2), (rows, 1), 0, top)
    return jnp.take_along_axis(listing, (jnp.arange(top)[None, :] + turn) % top, axis=1)


def shares(amount, total, reach, slope, full):
    portions = [(1 << 20) // math.isqrt(standing ** slope) + 1 for standing in range(1, amount + 1)]
    largest = reach if full else min(reach, max(-(-total // amount), total * portions[0] // sum(portions)))
    least = 1 if total - largest >= amount - 1 else 0
    holding, spare = [largest] + [least] * (amount - 1), total - largest - least * (amount - 1)
    while spare > 0:
        free = [i for i in range(1, amount) if holding[i] < largest] or [i for i in range(1, amount) if holding[i] < reach]
        pool, remaining = sum([portions[i] for i in free]), spare
        for i in free:
            more = min(reach - holding[i], max(1, remaining * portions[i] // pool), spare)
            holding[i] = holding[i] + more
            spare = spare - more
    return np.array(holding)


def bell_draw(rng, dims, width, limit, cuts=(), held_as=jnp.bfloat16):
    result = jax.random.normal(rng, dims, jnp.float32) * width
    if len(cuts) > 0:
        result = block_levels(rng, dims, cuts, -0.22, 0.18) * result
    return jnp.clip(result, min=-limit, max=limit).astype(held_as)


def setup_inputs(seed: int = 0) -> dict:
    splits = jax.random.split(jax.random.key(seed), 7)
    rhs = bell_draw(splits[0], (LEVELS, SUPERNODES, W, R), 1.0, 6.0, ((0, 8), (1, 32)))
    inverse_blocks = draw_inverse_blocks(jax.random.fold_in(splits[6], 71), 0)
    update_blocks = bell_draw(splits[2], (LEVELS, SUPERNODES, U, W), (2 * U) ** -0.5, 0.75, ((0, 8), (1, 32)))
    parent_owner_keys = jax.random.split(jax.random.fold_in(splits[3], 1), LEVELS * SUPERNODES // SN_DEV)
    parent_owner_turns = jax.random.permutation(jax.random.fold_in(splits[3], 3), LEVELS * SUPERNODES // SN_DEV)
    parent_owner = jax.vmap(lambda own, number: shared_out(jax.random.fold_in(splits[3], 2), own, number, SN_DEV, N_SUB, 1, CAP, 2))(parent_owner_keys, parent_owner_turns).reshape((LEVELS, SUPERNODES, 1))
    parent_slot = set_ends(jax.random.randint(splits[4], (LEVELS, SUPERNODES), 0, SN_DEV), jax.random.fold_in(splits[4], 1), 0, SN_DEV - 1).astype(jnp.int32)
    update_rows = draw_update_rows(jax.random.fold_in(splits[6], 71), 0)
    return {"rhs": rhs, "inverse_blocks": inverse_blocks, "update_blocks": update_blocks, "parent_owner": parent_owner, "parent_slot": parent_slot, "update_rows": update_rows}


def reference(rhs, inverse_blocks, update_blocks, parent_owner, parent_slot, update_rows):
    levels = rhs.shape[0]
    parents = (parent_owner[:, :, 0] * SN_DEV + parent_slot).astype(jnp.int32)
    accumulated = jnp.zeros(rhs.shape[1:], jnp.float32)
    forward = []
    for level_id in range(levels):
        shifted = (rhs[level_id].astype(jnp.float32) - accumulated).astype(jnp.bfloat16)
        solved = jnp.einsum("nvw,nwr->nvr", inverse_blocks[level_id].astype(jnp.float32), shifted.astype(jnp.float32)).astype(jnp.bfloat16)
        forward.append(solved)
        if level_id + 1 < levels:
            update = jnp.einsum("nuw,nwr->nur", update_blocks[level_id].astype(jnp.float32), solved.astype(jnp.float32)).astype(jnp.bfloat16)
            accumulated = jnp.zeros(rhs.shape[1:], jnp.float32).at[parents[level_id][:, None], update_rows[level_id]].add(update.astype(jnp.float32))
    solution = [None] * levels
    for level_id in reversed(range(levels)):
        if level_id + 1 < levels:
            replies = solution[level_id + 1][parents[level_id][:, None], update_rows[level_id]]
            lowered = forward[level_id].astype(jnp.float32) - jnp.einsum("nuw,nur->nwr", update_blocks[level_id].astype(jnp.float32), replies.astype(jnp.float32))
            backward = lowered.astype(jnp.bfloat16)
        else:
            backward = forward[level_id]
        solution[level_id] = jnp.einsum("nvw,nvr->nwr", inverse_blocks[level_id].astype(jnp.float32), backward.astype(jnp.float32)).astype(jnp.bfloat16)
    return jnp.stack(solution, axis=0)
```

```python
import functools
import jax
import jax.numpy as jnp
from jax import lax
from jax.experimental import pallas as pl
from jax.experimental.pallas import tpu as pltpu
from jax.sharding import Mesh
from jax.sharding import PartitionSpec as P

F32 = jnp.float32
BF16 = jnp.bfloat16
NN = (((1,), (0,)), ((), ()))
NT = (((1,), (1,)), ((), ()))
MB = 1 << 20


def dot(a, b, dims=NN):
    return lax.dot_general(a, b, dims, preferred_element_type=F32)


def four(block):
    return jnp.concatenate([block] * 4, axis=0)


def diagonal(height):
    rows = lax.broadcasted_iota(jnp.int32, (128, 128), 0)
    lanes = lax.broadcasted_iota(jnp.int32, (128, 128), 1)
    return rows // height == lanes // 32


def fold(square):
    kept = jnp.where(diagonal(32), square, 0.0)
    return kept[:32] + kept[32:64] + kept[64:96] + kept[96:]


def spread(flat):
    return jnp.where(diagonal(32), four(flat), 0.0).astype(BF16)


def reduce_kernel(
    place_ref, inverse_ref, rhs_ref, weights_ref, picks_ref, columns_ref, links_ref, reduced, staged
):
    step = pl.program_id(0)
    count = inverse_ref.shape[0]
    for k in range(count):
        n = step * count + k
        product = dot(weights_ref[k], inverse_ref[k]).astype(BF16)
        reduced[n] = product
        columns = fold(dot(rhs_ref[k].T, four(product), NT))
        staged[pl.ds(pl.multiple_of(n * 32, 32), 32), :] = columns

    @pl.when(step == pl.num_programs(0) - 1)
    def _():
        for q in range(32):
            columns_ref[q] = staged[pl.ds(q, 32, stride=32), :].astype(BF16)

        group = lax.broadcasted_iota(jnp.int32, (8, 128), 1) // 32

        def link(pair, carry):
            halves = []
            for r in range(2):
                slot = pair * 2 + r
                wide = dot(picks_ref[slot], four(reduced[place_ref[slot]]), NT)
                parts = [jnp.where(group == j, wide[j * 8 : j * 8 + 8], 0.0) for j in range(4)]
                halves.append(parts[0] + parts[1] + parts[2] + parts[3])
            links_ref[pair] = jnp.concatenate(halves, axis=0).astype(BF16)
            return carry

        lax.fori_loop(0, 32, link, 0, unroll=4)


def reduce_blocks(places, inverse, rhs, weights, picks):
    part = 8
    return pl.pallas_call(
        reduce_kernel,
        grid_spec=pltpu.PrefetchScalarGridSpec(
            num_scalar_prefetch=1,
            grid=(32 // part,),
            in_specs=[
                pl.BlockSpec((part, 256, 256), lambda s, p: (s, 0, 0)),
                pl.BlockSpec((part, 256, 128), lambda s, p: (s, 0, 0)),
                pl.BlockSpec((part, 32, 256), lambda s, p: (s, 0, 0)),
                pl.BlockSpec((64, 32, 256), lambda s, p: (0, 0, 0)),
            ],
            out_specs=[
                pl.BlockSpec((32, 32, 128), lambda s, p: (0, 0, 0)),
                pl.BlockSpec((32, 16, 128), lambda s, p: (0, 0, 0)),
            ],
            scratch_shapes=[pltpu.VMEM((32, 32, 256), BF16), pltpu.VMEM((1024, 128), F32)],
        ),
        out_shape=[
            jax.ShapeDtypeStruct((32, 32, 128), BF16),
            jax.ShapeDtypeStruct((32, 16, 128), BF16),
        ],
        compiler_params=pltpu.CompilerParams(vmem_limit_bytes=32 * MB),
        name="reduce_blocks",
    )(places, inverse, rhs, weights, picks)


def choose_kernel(place_ref, links_ref, out_ref, wide, staged):
    wide[...] = links_ref[...].astype(F32)
    for n in range(32):
        at = pl.multiple_of(place_ref[n] * 8, 8)
        staged[n * 8 : n * 8 + 8, :] = wide[pl.ds(at, 8), :]
    for j in range(8):
        out_ref[j] = staged[pl.ds(j, 32, stride=8), :].astype(BF16)


def choose_links(places, links):
    return pl.pallas_call(
        choose_kernel,
        in_specs=[
            pl.BlockSpec(memory_space=pltpu.SMEM),
            pl.BlockSpec(memory_space=pltpu.VMEM),
        ],
        out_specs=pl.BlockSpec(memory_space=pltpu.VMEM),
        scratch_shapes=[pltpu.VMEM((512, 128), F32), pltpu.VMEM((256, 128), F32)],
        out_shape=jax.ShapeDtypeStruct((8, 32, 128), BF16),
        name="choose_links",
    )(places, links)


def turn_kernel(x_ref, a_ref, b_ref, c_ref, d_ref, out_ref, staged):
    for distance, ref in enumerate((a_ref, b_ref, c_ref, d_ref)):
        at = pl.multiple_of((x_ref[0] + distance) % 4 * 32, 32)
        for j in range(8):
            staged[j, pl.ds(at, 32), :] = ref[j].astype(F32)
    for j in range(8):
        out_ref[j * 128 : j * 128 + 128, :] = staged[j].T.astype(BF16)


def turn_links(own_x, blocks):
    return pl.pallas_call(
        turn_kernel,
        in_specs=[pl.BlockSpec(memory_space=pltpu.SMEM)]
        + [pl.BlockSpec(memory_space=pltpu.VMEM)] * 4,
        out_specs=pl.BlockSpec(memory_space=pltpu.VMEM),
        scratch_shapes=[pltpu.VMEM((8, 128, 128), F32)],
        out_shape=jax.ShapeDtypeStruct((1024, 128), BF16),
        name="turn_links",
    )(own_x, *blocks)


def column_of(j8, j4):
    return j4 * 8 + j8


def multiply_links(lane0, links_ref, source, target):
    lanes = pl.ds(lane0, 128)
    for c in range(2):
        total = jnp.zeros((32, 128), F32)
        for j8 in range(8):
            for j4 in range(4):
                at = (j8 * 4 + j4) * 32
                row = source[pl.ds(c * 32 + column_of(j8, j4), 1), lanes]
                total = total + links_ref[at : at + 32, :].astype(F32) * row
        target[c * 32 : c * 32 + 32, lanes] = total


def multiply_links_turned(lane0, links_ref, source, target):
    lanes = pl.ds(lane0, 128)
    for c in range(2):
        column = source[c * 32 : c * 32 + 32, lanes]
        for j8 in range(8):
            for j4 in range(4):
                at = (j8 * 4 + j4) * 32
                product = links_ref[at : at + 32, :].astype(F32) * column
                row = jnp.sum(product, axis=0, keepdims=True)
                target[pl.ds(c * 32 + column_of(j8, j4), 1), lanes] = row


def each_block(place_ref, own_first, own, other, multiply, source, target):
    core = place_ref[1]

    def run(refs):
        for distance, ref in enumerate(refs):
            block = (place_ref[0] + distance) % 8
            multiply(pl.multiple_of(block * 128, 128), ref, source, target)

    pl.when(core == (0 if own_first else 1))(lambda: run(own))
    pl.when(core == (1 if own_first else 0))(lambda: run(other))


def down_kernel(place_ref, y_ref, ca_ref, cb_ref, ea_ref, eb_ref, *rest):
    own, other, (low_ref, high_ref, source, target) = rest[:8], rest[8:16], rest[16:]
    source[...] = y_ref[...].astype(F32)
    each_block(place_ref, True, own, other, multiply_links, source, target)
    low = ca_ref[...].astype(F32) - dot(target[...].astype(BF16), ea_ref[...])
    low = low.astype(BF16)
    low_ref[...] = low
    source[...] = low.astype(F32)
    each_block(place_ref, False, own, other, multiply_links, source, target)
    high = cb_ref[...].astype(F32) - dot(target[...].astype(BF16), eb_ref[...])
    high_ref[...] = high.astype(BF16)


def up_kernel(place_ref, z_ref, da_ref, db_ref, ea_ref, eb_ref, *rest):
    own, other, (high_ref, low_ref, source, target) = rest[:8], rest[8:16], rest[16:]
    source[...] = dot(z_ref[...], eb_ref[...], NT)
    each_block(place_ref, False, own, other, multiply_links_turned, source, target)
    high = (db_ref[...].astype(F32) - target[...]).astype(BF16)
    high_ref[...] = high
    source[...] = dot(high, ea_ref[...], NT)
    each_block(place_ref, True, own, other, multiply_links_turned, source, target)
    low_ref[...] = (da_ref[...].astype(F32) - target[...]).astype(BF16)


def chain_step(kernel, name, place, state, low, high, ea, eb, own, other):
    return pl.pallas_call(
        kernel,
        in_specs=[pl.BlockSpec(memory_space=pltpu.SMEM)]
        + [pl.BlockSpec(memory_space=pltpu.VMEM)] * 21,
        out_specs=[pl.BlockSpec(memory_space=pltpu.VMEM)] * 2,
        scratch_shapes=[pltpu.VMEM((64, 1024), F32)] * 2,
        out_shape=[jax.ShapeDtypeStruct((64, 1024), BF16)] * 2,
        compiler_params=pltpu.CompilerParams(vmem_limit_bytes=24 * MB),
        name=name,
    )(place, state, low, high, ea, eb, *own, *other)


def middle_kernel(
    place_ref, y_ref, inverse_ref, rhs_ref, picks_ref, forward_ref, d_ref, wide, added, solved, staged
):
    step = pl.program_id(0)
    count = inverse_ref.shape[0]

    @pl.when(step == 0)
    def _():
        added[...] = jnp.zeros_like(added)
        for q in range(32):
            wide[q * 64 : q * 64 + 64, :] = y_ref[q].astype(F32)

        def add(slot, carry):
            block = spread(wide[pl.ds(slot, 32, stride=64), :])
            place = place_ref[slot]
            added[place] = added[place] + dot(block, four(picks_ref[slot]))
            return carry

        lax.fori_loop(0, 64, add, 0, unroll=4)

    for k in range(count):
        n = step * count + k
        shifted = (rhs_ref[k].T.astype(F32) - added[n]).astype(BF16)
        forward = dot(shifted, inverse_ref[k], NT).astype(BF16)
        forward_ref[k] = forward
        solved[n] = dot(forward, inverse_ref[k]).astype(BF16)

    @pl.when(step == pl.num_programs(0) - 1)
    def _():
        def pick(slot, carry):
            block = fold(dot(solved[place_ref[slot]], four(picks_ref[slot]), NT))
            staged[pl.ds(pl.multiple_of(slot * 32, 32), 32), :] = block
            return carry

        lax.fori_loop(0, 64, pick, 0, unroll=4)
        for q in range(32):
            d_ref[q] = staged[pl.ds(q, 64, stride=32), :].astype(BF16)


def middle(places, y_items, inverse, rhs, picks):
    part = 8
    return pl.pallas_call(
        middle_kernel,
        grid_spec=pltpu.PrefetchScalarGridSpec(
            num_scalar_prefetch=1,
            grid=(32 // part,),
            in_specs=[
                pl.BlockSpec((32, 64, 128), lambda s, p: (0, 0, 0)),
                pl.BlockSpec((part, 256, 256), lambda s, p: (s, 0, 0)),
                pl.BlockSpec((part, 256, 128), lambda s, p: (s, 0, 0)),
                pl.BlockSpec((64, 32, 256), lambda s, p: (0, 0, 0)),
            ],
            out_specs=[
                pl.BlockSpec((part, 128, 256), lambda s, p: (s, 0, 0)),
                pl.BlockSpec((32, 64, 128), lambda s, p: (0, 0, 0)),
            ],
            scratch_shapes=[
                pltpu.VMEM((2048, 128), F32),
                pltpu.VMEM((32, 128, 256), F32),
                pltpu.VMEM((32, 128, 256), BF16),
                pltpu.VMEM((2048, 128), F32),
            ],
        ),
        out_shape=[
            jax.ShapeDtypeStruct((32, 128, 256), BF16),
            jax.ShapeDtypeStruct((32, 64, 128), BF16),
        ],
        compiler_params=pltpu.CompilerParams(vmem_limit_bytes=32 * MB),
        name="middle",
    )(places, y_items, inverse, rhs, picks)


def finish_kernel(z_ref, forward_ref, inverse_ref, weights_ref, out_ref, wide):
    step = pl.program_id(0)
    count = inverse_ref.shape[0]

    @pl.when(step == 0)
    def _():
        for q in range(32):
            wide[q * 32 : q * 32 + 32, :] = z_ref[q].astype(F32)

    for k in range(count):
        n = step * count + k
        block = spread(wide[pl.ds(n, 32, stride=32), :])
        lowered = forward_ref[k].astype(F32) - dot(block, four(weights_ref[k]))
        solved = dot(lowered.astype(BF16), inverse_ref[k])
        out_ref[k] = solved.T.astype(BF16)


def finish(z_items, forward, inverse, weights):
    part = 8
    return pl.pallas_call(
        finish_kernel,
        grid=(32 // part,),
        in_specs=[
            pl.BlockSpec((32, 32, 128), lambda s: (0, 0, 0)),
            pl.BlockSpec((part, 128, 256), lambda s: (s, 0, 0)),
            pl.BlockSpec((part, 256, 256), lambda s: (s, 0, 0)),
            pl.BlockSpec((part, 32, 256), lambda s: (s, 0, 0)),
        ],
        out_specs=pl.BlockSpec((part, 256, 128), lambda s: (s, 0, 0)),
        scratch_shapes=[pltpu.VMEM((1024, 128), F32)],
        out_shape=jax.ShapeDtypeStruct((32, 256, 128), BF16),
        compiler_params=pltpu.CompilerParams(vmem_limit_bytes=32 * MB),
        name="finish",
    )(z_items, forward, inverse, weights)


def ring(value, axis, distance):
    size = lax.axis_size(axis)
    return lax.ppermute(value, axis, [(i, (i + distance) % size) for i in range(size)])


def swap(value):
    return lax.ppermute(value, "core", [(0, 1), (1, 0)])


def hop(value, low):
    a, b = (low + 2) % 4, (low + 3) % 4
    return lax.ppermute(value, "y", [(low, low + 1), (low + 1, low), (a, b), (b, a)])


def across(value):
    return lax.all_to_all(value, ("z", "x"), split_axis=0, concat_axis=0, tiled=True)


def gather_links(block):
    ahead, behind = [block], [block]
    for _ in range(3):
        ahead.append(ring(ahead[-1], "z", -1))
        behind.append(ring(behind[-1], "z", 1))
    half = block.shape[0] // 2
    far = jnp.concatenate([ring(ahead[3][:half], "z", -1), ring(behind[3][half:], "z", 1)], axis=0)
    return [ahead[0], ahead[1], ahead[2], ahead[3], far, behind[3], behind[2], behind[1]]


def ranks_of(owners):
    by_sub = owners.reshape(32, 32)
    before = jnp.arange(32)[None, :] < jnp.arange(32)[:, None]
    same = (by_sub[:, :, None] == by_sub[:, None, :]) & before[None]
    return jnp.sum(same.astype(jnp.int32), axis=2).reshape(1024)


def on_device(rhs, inverse_blocks, update_blocks, parent_owner, parent_slot, update_rows):
    rhs, inverse, weights = rhs[0], inverse_blocks[0], update_blocks[0]
    z, x = lax.axis_index("z"), lax.axis_index("x")
    plane, core = lax.axis_index("y"), lax.axis_index("core")
    sub, level = z * 4 + x, plane * 2 + core

    def level_of(table, g):
        return lax.dynamic_index_in_dim(table, g, 0, keepdims=False)

    below = jnp.maximum(level - 1, 0)
    owners, slots = level_of(parent_owner[:, :, 0], below), level_of(parent_slot, below)
    rows = level_of(update_rows, below)
    ranks = ranks_of(owners)
    entry = jnp.arange(1024) // 32 * 2 + ranks
    is_child = (owners == sub) & (level > 0)
    hot = jnp.where(is_child[None, :] & (jnp.arange(64)[:, None] == entry[None, :]), 1.0, 0.0)
    listed = jnp.concatenate([rows, slots[:, None], jnp.ones_like(slots)[:, None]], axis=1)
    listed = dot(hot.astype(BF16), listed.astype(BF16))
    filled = listed[:, 33] > 0.5
    places = listed[:, 32].astype(jnp.int32)
    named = jnp.where(filled[:, None], listed[:, :32].astype(jnp.int32), -1)
    picks = (named[:, :, None] == jnp.arange(256)[None, None, :]).astype(BF16)

    send_columns, send_links = reduce_blocks(places, inverse, rhs, weights, picks)
    received = across(jnp.concatenate([send_links, send_columns], axis=1))
    own_entry = lax.dynamic_slice_in_dim(owners * 2 + ranks, sub * 32, 32)
    links = choose_links(own_entry, received[:, :16].reshape(512, 128))
    links = turn_links(x[None], [links, ring(links, "x", -1), ring(links, "x", 2), ring(links, "x", 1)])
    own_links = gather_links(links)
    other_links = [swap(block) for block in own_links]

    def halves(own):
        kept = jnp.where(core == 0, own[:64], own[64:])
        came = swap(jnp.where(core == 0, own[64:], own[:64]))
        return jnp.where(core == 0, kept, came), jnp.where(core == 0, came, kept)

    def wholes(low, high):
        kept, came = jnp.where(core == 0, low, high), swap(jnp.where(core == 0, high, low))
        first, second = jnp.where(core == 0, kept, came), jnp.where(core == 0, came, kept)
        return jnp.concatenate([first, second], axis=0)

    ca, cb = halves(received[:, 16:].reshape(1024, 128).T)

    def parents_of(g):
        names = level_of(parent_owner[:, :, 0], g) * 32 + level_of(parent_slot, g)
        return (names[:, None] == jnp.arange(1024)[None, :]).astype(BF16)

    ea = parents_of(jnp.maximum(plane * 2 - 1, 0))
    eb = parents_of(plane * 2)
    packing = (
        (owners * 64 + entry)[None, :] == jnp.arange(2048)[:, None]
    ).astype(BF16)

    place = jnp.stack([z, core])
    y_in = jnp.zeros((64, 1024), BF16)
    for step in range(4):
        low, high = chain_step(
            down_kernel, "down", place, y_in, ca, cb, ea, eb, own_links, other_links
        )
        if step < 3:
            y_in = jnp.where(plane == step + 1, hop(high, step), y_in)

    y_own = wholes(y_in, low)
    y_items = dot(packing, y_own, NT).astype(BF16)
    y_items = across(y_items.reshape(32, 64, 128))
    forward, d_items = middle(places, y_items, inverse, rhs, picks)
    d_items = across(d_items).reshape(2048, 128)
    d_own = lax.dot_general(
        d_items, packing, (((0,), (0,)), ((), ())), preferred_element_type=F32
    ).astype(BF16)
    da, db = halves(d_own)

    z_in = jnp.zeros((64, 1024), BF16)
    for step in reversed(range(4)):
        high, low = chain_step(
            up_kernel, "up", place, z_in, da, db, ea, eb, own_links, other_links
        )
        if step > 0:
            z_in = jnp.where(plane == step - 1, hop(low, step - 1), z_in)

    z_own = wholes(high, z_in)
    z_items = across(z_own.T.reshape(32, 32, 128))
    return finish(z_items, forward, inverse, weights)[None]


def solution(mesh):
    fine = Mesh(mesh.devices.reshape(8, 4, 4, 2), ("z", "x", "y", "core"))
    placed = P(("y", "core"), ("z", "x"), None, None)
    return jax.shard_map(
        on_device,
        mesh=fine,
        in_specs=(placed, placed, placed, P(), P(), P()),
        out_specs=placed,
        check_vma=False,
    )
```

```python
import functools
import jax
import jax.numpy as jnp
from jax import lax
from jax.experimental import pallas as pl
from jax.experimental.pallas import tpu as pltpu
from jax.sharding import Mesh
from jax.sharding import PartitionSpec as P

F32 = jnp.float32
BF16 = jnp.bfloat16
NN = (((1,), (0,)), ((), ()))
NT = (((1,), (1,)), ((), ()))
MB = 1 << 20


def dot(a, b, dims=NN):
    return lax.dot_general(a, b, dims, preferred_element_type=F32)


def four(block):
    return jnp.concatenate([block] * 4, axis=0)


def diagonal():
    rows = lax.broadcasted_iota(jnp.int32, (128, 128), 0)
    lanes = lax.broadcasted_iota(jnp.int32, (128, 128), 1)
    return rows // 32 == lanes // 32


def fold(square):
    kept = jnp.where(diagonal(), square, 0.0)
    return kept[:32] + kept[32:64] + kept[64:96] + kept[96:]


def spread(flat):
    return four(flat.astype(BF16)) * jnp.where(diagonal(), 1.0, 0.0).astype(BF16)


def reduce_kernel(
    place_ref, inverse_ref, rhs_ref, weights_ref, picks_ref, columns_ref, links_ref, reduced, staged
):
    step = pl.program_id(0)
    count = inverse_ref.shape[0]
    for k in range(count):
        n = step * count + k
        product = dot(weights_ref[k], inverse_ref[k]).astype(BF16)
        reduced[n] = product
        columns = fold(dot(rhs_ref[k].T, four(product), NT))
        staged[pl.ds(pl.multiple_of(n * 32, 32), 32), :] = columns

    @pl.when(step == pl.num_programs(0) - 1)
    def _():
        for q in range(32):
            columns_ref[q] = staged[pl.ds(q, 32, stride=32), :].astype(BF16)

        group = lax.broadcasted_iota(jnp.int32, (8, 128), 1) // 32

        def link(pair, carry):
            halves = []
            for r in range(2):
                slot = pair * 2 + r
                wide = dot(picks_ref[slot], four(reduced[place_ref[slot]]), NT)
                parts = [jnp.where(group == j, wide[j * 8 : j * 8 + 8], 0.0) for j in range(4)]
                halves.append(parts[0] + parts[1] + parts[2] + parts[3])
            links_ref[pair] = jnp.concatenate(halves, axis=0).astype(BF16)
            return carry

        lax.fori_loop(0, 32, link, 0, unroll=16)


def reduce_blocks(places, inverse, rhs, weights, picks):
    part = 8
    return pl.pallas_call(
        reduce_kernel,
        grid_spec=pltpu.PrefetchScalarGridSpec(
            num_scalar_prefetch=1,
            grid=(32 // part,),
            in_specs=[
                pl.BlockSpec((part, 256, 256), lambda s, p: (s, 0, 0)),
                pl.BlockSpec((part, 256, 128), lambda s, p: (s, 0, 0)),
                pl.BlockSpec((part, 32, 256), lambda s, p: (s, 0, 0)),
                pl.BlockSpec((64, 32, 256), lambda s, p: (0, 0, 0)),
            ],
            out_specs=[
                pl.BlockSpec((32, 32, 128), lambda s, p: (0, 0, 0)),
                pl.BlockSpec((32, 16, 128), lambda s, p: (0, 0, 0)),
            ],
            scratch_shapes=[pltpu.VMEM((32, 32, 256), BF16), pltpu.VMEM((1024, 128), F32)],
        ),
        out_shape=[
            jax.ShapeDtypeStruct((32, 32, 128), BF16),
            jax.ShapeDtypeStruct((32, 16, 128), BF16),
        ],
        compiler_params=pltpu.CompilerParams(vmem_limit_bytes=16 * MB),
        name="reduce_blocks",
    )(places, inverse, rhs, weights, picks)


def choose_kernel(place_ref, links_ref, out_ref, wide, staged):
    wide[...] = links_ref[...].astype(F32)
    for n in range(32):
        at = pl.multiple_of(place_ref[n] * 8, 8)
        staged[n * 8 : n * 8 + 8, :] = wide[pl.ds(at, 8), :]
    for j in range(8):
        out_ref[j] = staged[pl.ds(j, 32, stride=8), :].astype(BF16)


def choose_links(places, links):
    return pl.pallas_call(
        choose_kernel,
        in_specs=[
            pl.BlockSpec(memory_space=pltpu.SMEM),
            pl.BlockSpec(memory_space=pltpu.VMEM),
        ],
        out_specs=pl.BlockSpec(memory_space=pltpu.VMEM),
        scratch_shapes=[pltpu.VMEM((512, 128), F32), pltpu.VMEM((256, 128), F32)],
        out_shape=jax.ShapeDtypeStruct((8, 32, 128), BF16),
        compiler_params=pltpu.CompilerParams(vmem_limit_bytes=4 * MB),
        name="choose_links",
    )(places, links)


def turn_kernel(x_ref, a_ref, b_ref, c_ref, d_ref, out_ref, staged):
    for distance, ref in enumerate((a_ref, b_ref, c_ref, d_ref)):
        at = pl.multiple_of((x_ref[0] + distance) % 4 * 32, 32)
        for j in range(8):
            staged[j, pl.ds(at, 32), :] = ref[j].astype(F32)
    for j in range(8):
        out_ref[j * 128 : j * 128 + 128, :] = staged[j].T.astype(BF16)


def turn_links(own_x, blocks):
    return pl.pallas_call(
        turn_kernel,
        in_specs=[pl.BlockSpec(memory_space=pltpu.SMEM)]
        + [pl.BlockSpec(memory_space=pltpu.VMEM)] * 4,
        out_specs=pl.BlockSpec(memory_space=pltpu.VMEM),
        scratch_shapes=[pltpu.VMEM((8, 128, 128), F32)],
        out_shape=jax.ShapeDtypeStruct((1024, 128), BF16),
        compiler_params=pltpu.CompilerParams(vmem_limit_bytes=4 * MB),
        name="turn_links",
    )(own_x, *blocks)


def column_of(j8, j4):
    return j4 * 8 + j8


def multiply_links(lane0, links_ref, source, target):
    lanes = pl.ds(lane0, 128)
    for c in range(2):
        total = jnp.zeros((32, 128), F32)
        for j8 in range(8):
            for j4 in range(4):
                at = (j8 * 4 + j4) * 32
                row = source[pl.ds(c * 32 + column_of(j8, j4), 1), lanes]
                total = total + links_ref[at : at + 32, :].astype(F32) * row
        target[c * 32 : c * 32 + 32, lanes] = total


def multiply_links_turned(lane0, links_ref, source, target):
    lanes = pl.ds(lane0, 128)
    for c in range(2):
        column = source[c * 32 : c * 32 + 32, lanes]
        for j8 in range(8):
            for j4 in range(4):
                at = (j8 * 4 + j4) * 32
                product = links_ref[at : at + 32, :].astype(F32) * column
                row = jnp.sum(product, axis=0, keepdims=True)
                target[pl.ds(c * 32 + column_of(j8, j4), 1), lanes] = row


def collect_kernel(place_ref, names_ref, *rest):
    own, other, (links_ref, parents_ref, sems) = rest[:8], rest[8:16], rest[16:]

    def copies(first, second):
        return [
            pltpu.make_async_copy(refs[d], links_ref.at[which, d], sems.at[which, d])
            for which, refs in enumerate((first, second))
            for d in range(8)
        ]

    def start(first, second):
        for copy in copies(first, second):
            copy.start()

    pl.when(place_ref[0] == 0)(lambda: start(own, other))
    pl.when(place_ref[0] == 1)(lambda: start(other, own))
    lane = lax.broadcasted_iota(jnp.int32, (128, 1024), 1)
    for which in range(2):
        for block in range(8):
            column = names_ref[which : which + 1, block * 128 : block * 128 + 128].T
            parents_ref[which, block * 128 : block * 128 + 128, :] = jnp.where(
                lane == column, 1.0, 0.0
            ).astype(BF16)
    for copy in copies(own, other):
        copy.wait()


def collect(core, names, own, other):
    return pl.pallas_call(
        collect_kernel,
        in_specs=[
            pl.BlockSpec(memory_space=pltpu.SMEM),
            pl.BlockSpec(memory_space=pltpu.VMEM),
        ]
        + [pl.BlockSpec(memory_space=pl.ANY)] * 16,
        out_specs=[pl.BlockSpec(memory_space=pltpu.VMEM)] * 2,
        out_shape=[pltpu.VMEM((2, 8, 1024, 128), BF16), pltpu.VMEM((2, 1024, 1024), BF16)],
        scratch_shapes=[pltpu.SemaphoreType.DMA((2, 8))],
        compiler_params=pltpu.CompilerParams(vmem_limit_bytes=4 * MB),
        name="collect",
    )(core, names, *own, *other)


def each_block(place_ref, links_ref, which, multiply, source, target):
    for d in range(8):
        lane0 = pl.multiple_of((place_ref[0] + d) % 8 * 128, 128)
        multiply(lane0, links_ref.at[which, d], source, target)


def down_kernel(
    step,
    place_ref,
    kept_ref,
    came_ref,
    ca_ref,
    cb_ref,
    links_ref,
    parents_ref,
    state_ref,
    low_ref,
    high_ref,
    source,
    target,
):
    state = jnp.where(place_ref[2] == step, came_ref[...], kept_ref[...])
    state_ref[...] = state
    source[...] = state.astype(F32)
    each_block(place_ref, links_ref, 0, multiply_links, source, target)
    low = ca_ref[...].astype(F32) - dot(target[...].astype(BF16), parents_ref[0])
    low = low.astype(BF16)
    low_ref[...] = low
    source[...] = low.astype(F32)
    each_block(place_ref, links_ref, 1, multiply_links, source, target)
    high = cb_ref[...].astype(F32) - dot(target[...].astype(BF16), parents_ref[1])
    high_ref[...] = high.astype(BF16)


def up_kernel(
    step,
    place_ref,
    kept_ref,
    came_ref,
    da_ref,
    db_ref,
    links_ref,
    parents_ref,
    state_ref,
    low_ref,
    high_ref,
    source,
    target,
):
    state = jnp.where(place_ref[2] == step, came_ref[...], kept_ref[...])
    state_ref[...] = state
    source[...] = dot(state, parents_ref[1], NT)
    each_block(place_ref, links_ref, 1, multiply_links_turned, source, target)
    high = (db_ref[...].astype(F32) - target[...]).astype(BF16)
    high_ref[...] = high
    source[...] = dot(high, parents_ref[0], NT)
    each_block(place_ref, links_ref, 0, multiply_links_turned, source, target)
    low_ref[...] = (da_ref[...].astype(F32) - target[...]).astype(BF16)


def chain_step(kernel, name, step, place, kept, came, low, high, links, parents):
    links = pltpu.with_memory_space_constraint(links, pltpu.VMEM)
    parents = pltpu.with_memory_space_constraint(parents, pltpu.VMEM)
    return pl.pallas_call(
        functools.partial(kernel, step),
        in_specs=[pl.BlockSpec(memory_space=pltpu.SMEM)]
        + [pl.BlockSpec(memory_space=pltpu.VMEM)] * 6,
        out_specs=[pl.BlockSpec(memory_space=pltpu.VMEM)] * 3,
        scratch_shapes=[pltpu.VMEM((64, 1024), F32)] * 2,
        out_shape=[jax.ShapeDtypeStruct((64, 1024), BF16)] * 3,
        compiler_params=pltpu.CompilerParams(vmem_limit_bytes=8 * MB),
        name=name,
    )(place, kept, came, low, high, links, parents)


def middle_kernel(
    place_ref, y_ref, inverse_ref, rhs_ref, picks_ref, forward_ref, d_ref, wide, added, solved, staged
):
    step = pl.program_id(0)
    count = inverse_ref.shape[0]

    @pl.when(step == 0)
    def _():
        added[...] = jnp.zeros_like(added)
        for q in range(32):
            wide[q * 64 : q * 64 + 64, :] = y_ref[q].astype(F32)

        def add(slot, carry):
            block = spread(wide[pl.ds(slot, 32, stride=64), :])
            place = place_ref[slot]
            added[place] = added[place] + dot(block, four(picks_ref[slot]))
            return carry

        lax.fori_loop(0, 64, add, 0, unroll=16)

    for k in range(count):
        n = step * count + k
        shifted = (rhs_ref[k].T.astype(F32) - added[n]).astype(BF16)
        forward = dot(shifted, inverse_ref[k], NT).astype(BF16)
        forward_ref[k] = forward
        solved[n] = dot(forward, inverse_ref[k]).astype(BF16)

    @pl.when(step == pl.num_programs(0) - 1)
    def _():
        def pick(slot, carry):
            block = fold(dot(solved[place_ref[slot]], four(picks_ref[slot]), NT))
            staged[pl.ds(pl.multiple_of(slot * 32, 32), 32), :] = block
            return carry

        lax.fori_loop(0, 64, pick, 0, unroll=16)
        for q in range(32):
            d_ref[q] = staged[pl.ds(q, 64, stride=32), :].astype(BF16)


def middle(places, y_items, inverse, rhs, picks):
    part = 8
    return pl.pallas_call(
        middle_kernel,
        grid_spec=pltpu.PrefetchScalarGridSpec(
            num_scalar_prefetch=1,
            grid=(32 // part,),
            in_specs=[
                pl.BlockSpec((32, 64, 128), lambda s, p: (0, 0, 0)),
                pl.BlockSpec((part, 256, 256), lambda s, p: (s, 0, 0)),
                pl.BlockSpec((part, 256, 128), lambda s, p: (s, 0, 0)),
                pl.BlockSpec((64, 32, 256), lambda s, p: (0, 0, 0)),
            ],
            out_specs=[
                pl.BlockSpec((part, 128, 256), lambda s, p: (s, 0, 0)),
                pl.BlockSpec((32, 64, 128), lambda s, p: (0, 0, 0)),
            ],
            scratch_shapes=[
                pltpu.VMEM((2048, 128), F32),
                pltpu.VMEM((32, 128, 256), F32),
                pltpu.VMEM((32, 128, 256), BF16),
                pltpu.VMEM((2048, 128), F32),
            ],
        ),
        out_shape=[
            jax.ShapeDtypeStruct((32, 128, 256), BF16),
            jax.ShapeDtypeStruct((32, 64, 128), BF16),
        ],
        compiler_params=pltpu.CompilerParams(vmem_limit_bytes=24 * MB),
        name="middle",
    )(places, y_items, inverse, rhs, picks)


def finish_kernel(z_ref, forward_ref, inverse_ref, weights_ref, out_ref, wide):
    step = pl.program_id(0)
    count = inverse_ref.shape[0]

    @pl.when(step == 0)
    def _():
        for q in range(32):
            wide[q * 32 : q * 32 + 32, :] = z_ref[q].astype(F32)

    for k in range(count):
        n = step * count + k
        block = spread(wide[pl.ds(n, 32, stride=32), :])
        lowered = forward_ref[k].astype(F32) - dot(block, four(weights_ref[k]))
        solved = dot(lowered.astype(BF16), inverse_ref[k])
        out_ref[k] = solved.T.astype(BF16)


def finish(z_items, forward, inverse, weights):
    part = 8
    return pl.pallas_call(
        finish_kernel,
        grid=(32 // part,),
        in_specs=[
            pl.BlockSpec((32, 32, 128), lambda s: (0, 0, 0)),
            pl.BlockSpec((part, 128, 256), lambda s: (s, 0, 0)),
            pl.BlockSpec((part, 256, 256), lambda s: (s, 0, 0)),
            pl.BlockSpec((part, 32, 256), lambda s: (s, 0, 0)),
        ],
        out_specs=pl.BlockSpec((part, 256, 128), lambda s: (s, 0, 0)),
        scratch_shapes=[pltpu.VMEM((1024, 128), F32)],
        out_shape=jax.ShapeDtypeStruct((32, 256, 128), BF16),
        compiler_params=pltpu.CompilerParams(vmem_limit_bytes=16 * MB),
        name="finish",
    )(z_items, forward, inverse, weights)


def ring(value, axis, distance):
    size = lax.axis_size(axis)
    return lax.ppermute(value, axis, [(i, (i + distance) % size) for i in range(size)])


def swap(value):
    return lax.ppermute(value, "core", [(0, 1), (1, 0)])


def hop(value, low):
    a, b = (low + 2) % 4, (low + 3) % 4
    return lax.ppermute(value, "y", [(low, low + 1), (low + 1, low), (a, b), (b, a)])


def across(value):
    return lax.all_to_all(value, ("z", "x"), split_axis=0, concat_axis=0, tiled=True)


def gather_links(block):
    ahead, behind = [block], [block]
    for _ in range(3):
        ahead.append(ring(ahead[-1], "z", -1))
        behind.append(ring(behind[-1], "z", 1))
    half = block.shape[0] // 2
    far = jnp.concatenate([ring(ahead[3][:half], "z", -1), ring(behind[3][half:], "z", 1)], axis=0)
    return [ahead[0], ahead[1], ahead[2], ahead[3], far, behind[3], behind[2], behind[1]]


def ranks_of(owners):
    by_sub = owners.reshape(32, 32)
    before = jnp.arange(32)[None, :] < jnp.arange(32)[:, None]
    same = (by_sub[:, :, None] == by_sub[:, None, :]) & before[None]
    return jnp.sum(same.astype(jnp.int32), axis=2).reshape(1024)


def on_device(rhs, inverse_blocks, update_blocks, parent_owner, parent_slot, update_rows):
    rhs, inverse, weights = rhs[0], inverse_blocks[0], update_blocks[0]
    z, x = lax.axis_index("z"), lax.axis_index("x")
    plane, core = lax.axis_index("y"), lax.axis_index("core")
    sub, level = z * 4 + x, plane * 2 + core

    def level_of(table, g):
        return lax.dynamic_index_in_dim(table, g, 0, keepdims=False)

    below = jnp.maximum(level - 1, 0)
    owners, slots = level_of(parent_owner[:, :, 0], below), level_of(parent_slot, below)
    rows = level_of(update_rows, below)
    ranks = ranks_of(owners)
    entry = jnp.arange(1024) // 32 * 2 + ranks
    is_child = (owners == sub) & (level > 0)
    hot = jnp.where(is_child[None, :] & (jnp.arange(64)[:, None] == entry[None, :]), 1.0, 0.0)
    listed = jnp.concatenate([rows, slots[:, None], jnp.ones_like(slots)[:, None]], axis=1)
    listed = dot(hot.astype(BF16), listed.astype(BF16))
    filled = listed[:, 33] > 0.5
    places = listed[:, 32].astype(jnp.int32)
    named = jnp.where(filled[:, None], listed[:, :32].astype(jnp.int32), -1)
    picks = (named[:, :, None] == jnp.arange(256)[None, None, :]).astype(BF16)

    send_columns, send_links = reduce_blocks(places, inverse, rhs, weights, picks)
    received = across(jnp.concatenate([send_links, send_columns], axis=1))
    own_entry = lax.dynamic_slice_in_dim(owners * 2 + ranks, sub * 32, 32)
    links = choose_links(own_entry, received[:, :16].reshape(512, 128))
    links = turn_links(x[None], [links, ring(links, "x", -1), ring(links, "x", 2), ring(links, "x", 1)])
    own_links = gather_links(links)
    other_links = [swap(block) for block in own_links]

    def halves(own):
        kept = jnp.where(core == 0, own[:64], own[64:])
        came = swap(jnp.where(core == 0, own[64:], own[:64]))
        return jnp.where(core == 0, kept, came), jnp.where(core == 0, came, kept)

    def wholes(low, high):
        kept, came = jnp.where(core == 0, low, high), swap(jnp.where(core == 0, high, low))
        first, second = jnp.where(core == 0, kept, came), jnp.where(core == 0, came, kept)
        return jnp.concatenate([first, second], axis=0)

    ca, cb = halves(received[:, 16:].reshape(1024, 128).T)

    def parents_of(g):
        return level_of(parent_owner[:, :, 0], g) * 32 + level_of(parent_slot, g)

    names = jnp.stack([parents_of(jnp.maximum(plane * 2 - 1, 0)), parents_of(plane * 2)])
    links, parents = collect(core[None], names, own_links, other_links)
    packing = (
        (owners * 64 + entry)[None, :] == jnp.arange(2048)[:, None]
    ).astype(BF16)

    place = jnp.stack([z, core, plane])
    zeros = jnp.zeros((64, 1024), BF16)
    y_in = came = zeros
    for step in range(4):
        y_in, low, high = chain_step(
            down_kernel, "down", step, place, y_in, came, ca, cb, links, parents
        )
        if step < 3:
            came = hop(high, step)

    y_own = wholes(y_in, low)
    y_items = dot(packing, y_own, NT).astype(BF16)
    y_items = across(y_items.reshape(32, 64, 128))
    forward, d_items = middle(places, y_items, inverse, rhs, picks)
    d_items = across(d_items).reshape(2048, 128)
    d_own = lax.dot_general(
        d_items, packing, (((0,), (0,)), ((), ())), preferred_element_type=F32
    ).astype(BF16)
    da, db = halves(d_own)

    z_in = came = zeros
    for step in reversed(range(4)):
        z_in, low, high = chain_step(
            up_kernel, "up", step, place, z_in, came, da, db, links, parents
        )
        if step > 0:
            came = hop(low, step - 1)

    z_own = wholes(high, z_in)
    z_items = across(z_own.T.reshape(32, 32, 128))
    return finish(z_items, forward, inverse, weights)[None]


def solution(mesh):
    fine = Mesh(mesh.devices.reshape(8, 4, 4, 2), ("z", "x", "y", "core"))
    placed = P(("y", "core"), ("z", "x"), None, None)
    return jax.shard_map(
        on_device,
        mesh=fine,
        in_specs=(placed, placed, placed, P(), P(), P()),
        out_specs=placed,
        check_vma=False,
    )
```

```python
import functools
import jax
import jax.numpy as jnp
from jax import lax
from jax.experimental import pallas as pl
from jax.experimental.pallas import tpu as pltpu
from jax.sharding import Mesh
from jax.sharding import PartitionSpec as P

F32 = jnp.float32
BF16 = jnp.bfloat16
NN = (((1,), (0,)), ((), ()))
NT = (((1,), (1,)), ((), ()))
MB = 1 << 20


def dot(a, b, dims=NN):
    return lax.dot_general(a, b, dims, preferred_element_type=F32)


def four(block):
    return jnp.concatenate([block] * 4, axis=0)


def diagonal():
    rows = lax.broadcasted_iota(jnp.int32, (128, 128), 0)
    lanes = lax.broadcasted_iota(jnp.int32, (128, 128), 1)
    return rows // 32 == lanes // 32


def fold(square):
    kept = jnp.where(diagonal(), square, 0.0)
    return kept[:32] + kept[32:64] + kept[64:96] + kept[96:]


def spread(flat):
    return four(flat.astype(BF16)) * jnp.where(diagonal(), 1.0, 0.0).astype(BF16)


def first_half(place_ref, block):
    other = jnp.concatenate([block[64:], block[:64]], axis=0)
    return jnp.where(place_ref[64] == 0, block, other)


def reduce_kernel(
    place_ref, inverse_ref, rhs_ref, weights_ref, picks_ref, out_ref, reduced, staged
):
    step = pl.program_id(0)
    count = inverse_ref.shape[0]
    for k in range(count):
        n = step * count + k
        product = dot(weights_ref[k], inverse_ref[k]).astype(BF16)
        reduced[n] = product
        columns = fold(dot(first_half(place_ref, rhs_ref[k].T), four(product), NT))
        staged[pl.ds(pl.multiple_of(n * 32, 32), 32), :] = columns

    @pl.when(step == pl.num_programs(0) - 1)
    def _():
        for q in range(32):
            out_ref[q, 16:48, :] = staged[pl.ds(q, 32, stride=32), :].astype(BF16)

        group = lax.broadcasted_iota(jnp.int32, (8, 128), 1) // 32

        def link(pair, carry):
            halves = []
            for r in range(2):
                slot = pair * 2 + r
                wide = dot(picks_ref[slot], four(reduced[place_ref[slot]]), NT)
                parts = [jnp.where(group == j, wide[j * 8 : j * 8 + 8], 0.0) for j in range(4)]
                halves.append(parts[0] + parts[1] + parts[2] + parts[3])
            out_ref[pair, 0:16, :] = jnp.concatenate(halves, axis=0).astype(BF16)
            return carry

        lax.fori_loop(0, 32, link, 0, unroll=16)


def reduce_blocks(places, inverse, rhs, weights, picks):
    part = 8
    return pl.pallas_call(
        reduce_kernel,
        grid_spec=pltpu.PrefetchScalarGridSpec(
            num_scalar_prefetch=1,
            grid=(32 // part,),
            in_specs=[
                pl.BlockSpec((part, 256, 256), lambda s, p: (s, 0, 0)),
                pl.BlockSpec((part, 256, 128), lambda s, p: (s, 0, 0)),
                pl.BlockSpec((part, 32, 256), lambda s, p: (s, 0, 0)),
                pl.BlockSpec((64, 32, 256), lambda s, p: (0, 0, 0)),
            ],
            out_specs=pl.BlockSpec((32, 48, 128), lambda s, p: (0, 0, 0)),
            scratch_shapes=[pltpu.VMEM((32, 32, 256), BF16), pltpu.VMEM((1024, 128), F32)],
        ),
        out_shape=jax.ShapeDtypeStruct((32, 48, 128), BF16),
        compiler_params=pltpu.CompilerParams(vmem_limit_bytes=16 * MB),
        name="reduce_blocks",
    )(places, inverse, rhs, weights, picks)


def choose_kernel(place_ref, received_ref, links_ref, kept_ref, sent_ref, wide, staged):
    for t in range(32):
        wide[t * 16 : t * 16 + 16, :] = received_ref[t, 0:16, :].astype(F32)
    for n in range(32):
        at = pl.multiple_of(place_ref[n] * 8, 8)
        staged[n * 8 : n * 8 + 8, :] = wide[pl.ds(at, 8), :]
    for j in range(8):
        links_ref[j] = staged[pl.ds(j, 32, stride=8), :].astype(BF16)
    for block in range(8):
        rows = [received_ref[block * 4 + s, 16:48, :].astype(F32) for s in range(4)]
        turned = jnp.concatenate(rows, axis=0).T
        lanes = slice(block * 128, block * 128 + 128)
        kept_ref[:, lanes] = turned[:64].astype(BF16)
        sent_ref[:, lanes] = turned[64:].astype(BF16)


def choose_links(places, received):
    return pl.pallas_call(
        choose_kernel,
        in_specs=[
            pl.BlockSpec(memory_space=pltpu.SMEM),
            pl.BlockSpec(memory_space=pltpu.VMEM),
        ],
        out_specs=[pl.BlockSpec(memory_space=pltpu.VMEM)] * 3,
        scratch_shapes=[pltpu.VMEM((512, 128), F32), pltpu.VMEM((256, 128), F32)],
        out_shape=[jax.ShapeDtypeStruct((8, 32, 128), BF16)]
        + [jax.ShapeDtypeStruct((64, 1024), BF16)] * 2,
        compiler_params=pltpu.CompilerParams(vmem_limit_bytes=4 * MB),
        name="choose_links",
    )(places, received)


def turn_kernel(x_ref, a_ref, b_ref, c_ref, d_ref, out_ref, staged):
    for distance, ref in enumerate((a_ref, b_ref, c_ref, d_ref)):
        at = pl.multiple_of((x_ref[0] + distance) % 4 * 32, 32)
        for j in range(8):
            staged[j, pl.ds(at, 32), :] = ref[j].astype(F32)
    for j in range(8):
        out_ref[j * 128 : j * 128 + 128, :] = staged[j].T.astype(BF16)


def turn_links(own_x, blocks):
    return pl.pallas_call(
        turn_kernel,
        in_specs=[pl.BlockSpec(memory_space=pltpu.SMEM)]
        + [pl.BlockSpec(memory_space=pltpu.VMEM)] * 4,
        out_specs=pl.BlockSpec(memory_space=pltpu.VMEM),
        scratch_shapes=[pltpu.VMEM((8, 128, 128), F32)],
        out_shape=jax.ShapeDtypeStruct((1024, 128), BF16),
        compiler_params=pltpu.CompilerParams(vmem_limit_bytes=4 * MB),
        name="turn_links",
    )(own_x, *blocks)


def column_of(j8, j4):
    return j4 * 8 + j8


def collect_kernel(place_ref, names_ref, *rest):
    own, other, (links_ref, parents_ref, sems) = rest[:8], rest[8:16], rest[16:]

    def copies(first, second):
        return [
            pltpu.make_async_copy(refs[d], links_ref.at[which, d], sems.at[which, d])
            for which, refs in enumerate((first, second))
            for d in range(8)
        ]

    def start(first, second):
        for copy in copies(first, second):
            copy.start()

    pl.when(place_ref[0] == 0)(lambda: start(own, other))
    pl.when(place_ref[0] == 1)(lambda: start(other, own))
    lane = lax.broadcasted_iota(jnp.int32, (128, 1024), 1)
    for which in range(2):
        for block in range(8):
            column = names_ref[which : which + 1, block * 128 : block * 128 + 128].T
            parents_ref[which, block * 128 : block * 128 + 128, :] = jnp.where(
                lane == column, 1.0, 0.0
            ).astype(BF16)
    for copy in copies(own, other):
        copy.wait()


def collect(core, names, own, other):
    return pl.pallas_call(
        collect_kernel,
        in_specs=[
            pl.BlockSpec(memory_space=pltpu.SMEM),
            pl.BlockSpec(memory_space=pltpu.VMEM),
        ]
        + [pl.BlockSpec(memory_space=pl.ANY)] * 16,
        out_specs=[pl.BlockSpec(memory_space=pltpu.VMEM)] * 2,
        out_shape=[pltpu.VMEM((2, 8, 1024, 128), BF16), pltpu.VMEM((2, 1024, 1024), BF16)],
        scratch_shapes=[pltpu.SemaphoreType.DMA((2, 8))],
        compiler_params=pltpu.CompilerParams(vmem_limit_bytes=4 * MB),
        name="collect",
    )(core, names, *own, *other)


def multiply_links(lane0, links_ref, source, target):
    lanes = pl.ds(lane0, 128)
    totals = [jnp.zeros((32, 128), F32)] * 2
    for j8 in range(8):
        for j4 in range(4):
            at = (j8 * 4 + j4) * 32
            link = links_ref[at : at + 32, :].astype(F32)
            for c in range(2):
                row = source[pl.ds(c * 32 + column_of(j8, j4), 1), lanes]
                totals[c] = totals[c] + link * row
    for c in range(2):
        target[c * 32 : c * 32 + 32, lanes] = totals[c]


def multiply_links_turned(lane0, links_ref, source, target):
    lanes = pl.ds(lane0, 128)
    columns = [source[c * 32 : c * 32 + 32, lanes] for c in range(2)]
    for j8 in range(8):
        for j4 in range(4):
            at = (j8 * 4 + j4) * 32
            link = links_ref[at : at + 32, :].astype(F32)
            for c in range(2):
                row = jnp.sum(link * columns[c], axis=0, keepdims=True)
                target[pl.ds(c * 32 + column_of(j8, j4), 1), lanes] = row


def by_level(place_ref, kept_ref, came_ref):
    kept, came = kept_ref[...].astype(F32), came_ref[...].astype(F32)
    first = place_ref[1] == 0
    return jnp.where(first, kept, came), jnp.where(first, came, kept)


def gather_parents(names_ref, which, state):
    state = state.astype(F32)
    blocks = [state[:, s * 128 : s * 128 + 128] for s in range(8)]
    chosen = []
    for block in range(8):
        names = names_ref[which : which + 1, block * 128 : block * 128 + 128]
        lane = jnp.broadcast_to(names % 128, (64, 128))
        tile = jnp.broadcast_to(names // 128, (64, 128))
        total = jnp.zeros((64, 128), F32)
        for s in range(8):
            found = jnp.take_along_axis(blocks[s], lane, axis=1, mode="promise_in_bounds")
            total = jnp.where(tile == s, found, total)
        chosen.append(total)
    return jnp.concatenate(chosen, axis=1)


def share(place_ref, first, second, kept_ref, sent_ref):
    kept_ref[...] = jnp.where(place_ref[1] == 0, first, second)
    sent_ref[...] = jnp.where(place_ref[1] == 0, second, first)


def each_block(place_ref, links_ref, which, multiply, source, target):
    for d in range(8):
        lane0 = pl.multiple_of((place_ref[0] + d) % 8 * 128, 128)
        multiply(lane0, links_ref.at[which, d], source, target)


def down_kernel(
    step,
    place_ref,
    kept_ref,
    came_ref,
    own_ref,
    other_ref,
    links_ref,
    parents_ref,
    state_ref,
    next_ref,
    kept_out_ref,
    sent_out_ref,
    source,
    target,
):
    state = jnp.where(place_ref[2] == step, came_ref[...], kept_ref[...])
    state_ref[...] = state
    source[...] = state.astype(F32)
    each_block(place_ref, links_ref, 0, multiply_links, source, target)
    even, odd = by_level(place_ref, own_ref, other_ref)
    low = even - dot(target[...].astype(BF16), parents_ref[0])
    low = low.astype(BF16)
    share(place_ref, state, low, kept_out_ref, sent_out_ref)
    source[...] = low.astype(F32)
    each_block(place_ref, links_ref, 1, multiply_links, source, target)
    high = odd - dot(target[...].astype(BF16), parents_ref[1])
    next_ref[...] = high.astype(BF16)


def up_kernel(
    step,
    place_ref,
    kept_ref,
    came_ref,
    own_ref,
    other_ref,
    links_ref,
    parents_ref,
    state_ref,
    next_ref,
    kept_out_ref,
    sent_out_ref,
    source,
    target,
):
    state = jnp.where(place_ref[2] == step, came_ref[...], kept_ref[...])
    state_ref[...] = state
    source[...] = gather_parents(parents_ref, 1, state)
    each_block(place_ref, links_ref, 1, multiply_links_turned, source, target)
    even, odd = by_level(place_ref, own_ref, other_ref)
    high = (odd - target[...]).astype(BF16)
    share(place_ref, high, state, kept_out_ref, sent_out_ref)
    source[...] = gather_parents(parents_ref, 0, high)
    each_block(place_ref, links_ref, 0, multiply_links_turned, source, target)
    next_ref[...] = (even - target[...]).astype(BF16)


def chain_step(kernel, name, step, place, kept, came, low, high, links, parents):
    links = pltpu.with_memory_space_constraint(links, pltpu.VMEM)
    return pl.pallas_call(
        functools.partial(kernel, step),
        in_specs=[pl.BlockSpec(memory_space=pltpu.SMEM)]
        + [pl.BlockSpec(memory_space=pltpu.VMEM)] * 6,
        out_specs=[pl.BlockSpec(memory_space=pltpu.VMEM)] * 4,
        scratch_shapes=[pltpu.VMEM((64, 1024), F32)] * 2,
        out_shape=[jax.ShapeDtypeStruct((64, 1024), BF16)] * 4,
        compiler_params=pltpu.CompilerParams(vmem_limit_bytes=8 * MB),
        name=name,
    )(place, kept, came, low, high, links, parents)


def middle_kernel(
    place_ref, y_ref, inverse_ref, rhs_ref, picks_ref, forward_ref, d_ref, wide, added, solved, staged
):
    step = pl.program_id(0)
    count = inverse_ref.shape[0]

    @pl.when(step == 0)
    def _():
        added[...] = jnp.zeros_like(added)
        for q in range(32):
            wide[q * 64 : q * 64 + 64, :] = y_ref[q].astype(F32)

        def add(slot, carry):
            block = spread(wide[pl.ds(slot, 32, stride=64), :])
            place = place_ref[slot]
            added[place] = added[place] + dot(block, four(picks_ref[slot]))
            return carry

        lax.fori_loop(0, 64, add, 0, unroll=16)

    for k in range(count):
        n = step * count + k
        shifted = (first_half(place_ref, rhs_ref[k].T).astype(F32) - added[n]).astype(BF16)
        forward = dot(shifted, inverse_ref[k], NT).astype(BF16)
        forward_ref[k] = forward
        solved[n] = dot(forward, inverse_ref[k]).astype(BF16)

    @pl.when(step == pl.num_programs(0) - 1)
    def _():
        def pick(slot, carry):
            block = fold(dot(solved[place_ref[slot]], four(picks_ref[slot]), NT))
            staged[pl.ds(pl.multiple_of(slot * 32, 32), 32), :] = block
            return carry

        lax.fori_loop(0, 64, pick, 0, unroll=16)
        for q in range(32):
            d_ref[q] = staged[pl.ds(q, 64, stride=32), :].astype(BF16)


def middle(places, y_items, inverse, rhs, picks):
    part = 8
    return pl.pallas_call(
        middle_kernel,
        grid_spec=pltpu.PrefetchScalarGridSpec(
            num_scalar_prefetch=1,
            grid=(32 // part,),
            in_specs=[
                pl.BlockSpec((32, 64, 128), lambda s, p: (0, 0, 0)),
                pl.BlockSpec((part, 256, 256), lambda s, p: (s, 0, 0)),
                pl.BlockSpec((part, 256, 128), lambda s, p: (s, 0, 0)),
                pl.BlockSpec((64, 32, 256), lambda s, p: (0, 0, 0)),
            ],
            out_specs=[
                pl.BlockSpec((part, 128, 256), lambda s, p: (s, 0, 0)),
                pl.BlockSpec((32, 64, 128), lambda s, p: (0, 0, 0)),
            ],
            scratch_shapes=[
                pltpu.VMEM((2048, 128), F32),
                pltpu.VMEM((32, 128, 256), F32),
                pltpu.VMEM((32, 128, 256), BF16),
                pltpu.VMEM((2048, 128), F32),
            ],
        ),
        out_shape=[
            jax.ShapeDtypeStruct((32, 128, 256), BF16),
            jax.ShapeDtypeStruct((32, 64, 128), BF16),
        ],
        compiler_params=pltpu.CompilerParams(vmem_limit_bytes=24 * MB),
        name="middle",
    )(places, y_items, inverse, rhs, picks)


def finish_kernel(place_ref, z_ref, forward_ref, inverse_ref, weights_ref, out_ref, wide):
    step = pl.program_id(0)
    count = inverse_ref.shape[0]

    @pl.when(step == 0)
    def _():
        for q in range(32):
            wide[q * 32 : q * 32 + 32, :] = z_ref[q].astype(F32)

    for k in range(count):
        n = step * count + k
        block = spread(wide[pl.ds(n, 32, stride=32), :])
        lowered = forward_ref[k].astype(F32) - dot(block, four(weights_ref[k]))
        solved = dot(lowered.astype(BF16), inverse_ref[k])
        out_ref[k] = first_half(place_ref, solved).T.astype(BF16)


def finish(places, z_items, forward, inverse, weights):
    part = 8
    return pl.pallas_call(
        finish_kernel,
        grid=(32 // part,),
        in_specs=[
            pl.BlockSpec(memory_space=pltpu.SMEM),
            pl.BlockSpec((32, 32, 128), lambda s: (0, 0, 0)),
            pl.BlockSpec((part, 128, 256), lambda s: (s, 0, 0)),
            pl.BlockSpec((part, 256, 256), lambda s: (s, 0, 0)),
            pl.BlockSpec((part, 32, 256), lambda s: (s, 0, 0)),
        ],
        out_specs=pl.BlockSpec((part, 256, 128), lambda s: (s, 0, 0)),
        scratch_shapes=[pltpu.VMEM((1024, 128), F32)],
        out_shape=jax.ShapeDtypeStruct((32, 256, 128), BF16),
        compiler_params=pltpu.CompilerParams(vmem_limit_bytes=16 * MB),
        name="finish",
    )(places, z_items, forward, inverse, weights)


def ring(value, axis, distance):
    size = lax.axis_size(axis)
    return lax.ppermute(value, axis, [(i, (i + distance) % size) for i in range(size)])


def swap(value):
    return lax.ppermute(value, "core", [(0, 1), (1, 0)])


def hop(value, low):
    a, b = (low + 2) % 4, (low + 3) % 4
    return lax.ppermute(value, "y", [(low, low + 1), (low + 1, low), (a, b), (b, a)])


def across(value):
    return lax.all_to_all(value, ("z", "x"), split_axis=0, concat_axis=0, tiled=True)


def gather_links(block):
    ahead, behind = [block], [block]
    for _ in range(3):
        ahead.append(ring(ahead[-1], "z", -1))
        behind.append(ring(behind[-1], "z", 1))
    far = ring(ahead[3], "z", -1)
    return [ahead[0], ahead[1], ahead[2], ahead[3], far, behind[3], behind[2], behind[1]]


def ranks_of(owners):
    by_sub = owners.reshape(32, 32)
    before = jnp.arange(32)[None, :] < jnp.arange(32)[:, None]
    same = (by_sub[:, :, None] == by_sub[:, None, :]) & before[None]
    return jnp.sum(same.astype(jnp.int32), axis=2).reshape(1024)


def on_device(rhs, inverse_blocks, update_blocks, parent_owner, parent_slot, update_rows):
    rhs, inverse, weights = rhs[0], inverse_blocks[0], update_blocks[0]
    z, x = lax.axis_index("z"), lax.axis_index("x")
    plane, core = lax.axis_index("y"), lax.axis_index("core")
    sub, level = z * 4 + x, plane * 2 + core

    def level_of(table, g):
        return lax.dynamic_index_in_dim(table, g, 0, keepdims=False)

    below = jnp.maximum(level - 1, 0)
    owners, slots = level_of(parent_owner[:, :, 0], below), level_of(parent_slot, below)
    rows = level_of(update_rows, below)
    ranks = ranks_of(owners)
    entry = jnp.arange(1024) // 32 * 2 + ranks
    is_child = (owners == sub) & (level > 0)
    hot = jnp.where(is_child[None, :] & (jnp.arange(64)[:, None] == entry[None, :]), 1.0, 0.0)
    listed = jnp.concatenate([rows, slots[:, None], jnp.ones_like(slots)[:, None]], axis=1)
    listed = dot(hot.astype(BF16), listed.astype(BF16))
    filled = listed[:, 33] > 0.5
    places = jnp.concatenate([listed[:, 32].astype(jnp.int32), core[None]])
    named = jnp.where(filled[:, None], listed[:, :32].astype(jnp.int32), -1)
    picks = (named[:, :, None] == jnp.arange(256)[None, None, :]).astype(BF16)

    received = across(reduce_blocks(places, inverse, rhs, weights, picks))
    own_entry = lax.dynamic_slice_in_dim(owners * 2 + ranks, sub * 32, 32)
    links, c_own, c_sent = choose_links(own_entry, received)
    c_other = swap(c_sent)
    links = turn_links(x[None], [links, ring(links, "x", -1), ring(links, "x", 2), ring(links, "x", 1)])
    own_links = gather_links(links)
    other_links = [swap(block) for block in own_links]

    def parents_of(g):
        return level_of(parent_owner[:, :, 0], g) * 32 + level_of(parent_slot, g)

    names = jnp.stack([parents_of(jnp.maximum(plane * 2 - 1, 0)), parents_of(plane * 2)])
    links, parents = collect(core[None], names, own_links, other_links)
    packing = (
        (owners * 64 + entry)[None, :] == jnp.arange(2048)[:, None]
    ).astype(BF16)

    place = jnp.stack([z, core, plane])
    zeros = jnp.zeros((64, 1024), BF16)
    held = pltpu.with_memory_space_constraint(parents, pltpu.VMEM)
    y_in = came = zeros
    for step in range(4):
        y_in, leaving, kept, sent = chain_step(
            down_kernel, "down", step, place, y_in, came, c_own, c_other, links, held
        )
        if step < 3:
            came = hop(leaving, step)

    y_own = jnp.concatenate([kept, swap(sent)], axis=0)
    y_items = dot(packing, y_own, NT).astype(BF16)
    y_items = across(y_items.reshape(32, 64, 128))
    forward, d_items = middle(places, y_items, inverse, rhs, picks)
    d_items = across(d_items).reshape(2048, 128)
    d_own = lax.dot_general(
        d_items, packing, (((0,), (0,)), ((), ())), preferred_element_type=F32
    ).astype(BF16)
    d_own, d_other = d_own[:64], swap(d_own[64:])

    z_in = came = zeros
    for step in reversed(range(4)):
        z_in, leaving, kept, sent = chain_step(
            up_kernel, "up", step, place, z_in, came, d_own, d_other, links, names
        )
        if step > 0:
            came = hop(leaving, step - 1)

    z_own = jnp.concatenate([kept, swap(sent)], axis=0)
    z_items = across(z_own.T.reshape(32, 32, 128))
    return finish(places, z_items, forward, inverse, weights)[None]


def solution(mesh):
    fine = Mesh(mesh.devices.reshape(8, 4, 4, 2), ("z", "x", "y", "core"))
    placed = P(("y", "core"), ("z", "x"), None, None)
    return jax.shard_map(
        on_device,
        mesh=fine,
        in_specs=(placed, placed, placed, P(), P(), P()),
        out_specs=placed,
        check_vma=False,
    )
```

```python
import functools
import jax
import jax.numpy as jnp
from jax import lax
from jax.experimental import pallas as pl
from jax.experimental.pallas import tpu as pltpu
from jax.sharding import Mesh
from jax.sharding import PartitionSpec as P

F32 = jnp.float32
BF16 = jnp.bfloat16
NN = (((1,), (0,)), ((), ()))
NT = (((1,), (1,)), ((), ()))
MB = 1 << 20


def dot(a, b, dims=NN):
    return lax.dot_general(a, b, dims, preferred_element_type=F32)


def four(block):
    return jnp.concatenate([block] * 4, axis=0)


def diagonal():
    rows = lax.broadcasted_iota(jnp.int32, (128, 128), 0)
    lanes = lax.broadcasted_iota(jnp.int32, (128, 128), 1)
    return rows // 32 == lanes // 32


def fold(square):
    kept = jnp.where(diagonal(), square, 0.0)
    return kept[:32] + kept[32:64] + kept[64:96] + kept[96:]


def spread(flat):
    return four(flat.astype(BF16)) * jnp.where(diagonal(), 1.0, 0.0).astype(BF16)


def first_half(place_ref, block):
    other = jnp.concatenate([block[64:], block[:64]], axis=0)
    return jnp.where(place_ref[64] == 0, block, other)


def reduce_kernel(
    place_ref, inverse_ref, rhs_ref, weights_ref, listed_ref, out_ref, picks_ref, reduced, staged
):
    step = pl.program_id(0)
    count = inverse_ref.shape[0]

    @pl.when(step == 0)
    def _():
        named = listed_ref[:, 0:128].T[:32]
        filled = listed_ref[:, 128:256].T[1:2]
        named = jnp.where(filled > 0.5, named, -1.0).astype(jnp.int32)
        lane = lax.broadcasted_iota(jnp.int32, (32, 256), 1)
        for slot in range(64):
            hit = jnp.broadcast_to(named[:, slot : slot + 1], (32, 256)) == lane
            picks_ref[slot] = jnp.where(hit, 1.0, 0.0).astype(BF16)

    for k in range(count):
        n = step * count + k
        product = dot(weights_ref[k], inverse_ref[k]).astype(BF16)
        reduced[n] = product
        columns = fold(dot(first_half(place_ref, rhs_ref[k].T), four(product), NT))
        staged[pl.ds(pl.multiple_of(n * 32, 32), 32), :] = columns

    @pl.when(step == pl.num_programs(0) - 1)
    def _():
        for q in range(32):
            out_ref[q, 16:48, :] = staged[pl.ds(q, 32, stride=32), :].astype(BF16)

        group = lax.broadcasted_iota(jnp.int32, (8, 128), 1) // 32

        def link(pair, carry):
            halves = []
            for r in range(2):
                slot = pair * 2 + r
                wide = dot(picks_ref[slot], four(reduced[place_ref[slot]]), NT)
                parts = [jnp.where(group == j, wide[j * 8 : j * 8 + 8], 0.0) for j in range(4)]
                halves.append(parts[0] + parts[1] + parts[2] + parts[3])
            out_ref[pair, 0:16, :] = jnp.concatenate(halves, axis=0).astype(BF16)
            return carry

        lax.fori_loop(0, 32, link, 0, unroll=16)


def reduce_blocks(places, inverse, rhs, weights, listed):
    part = 8
    return pl.pallas_call(
        reduce_kernel,
        grid_spec=pltpu.PrefetchScalarGridSpec(
            num_scalar_prefetch=1,
            grid=(32 // part,),
            in_specs=[
                pl.BlockSpec((part, 256, 256), lambda s, p: (s, 0, 0)),
                pl.BlockSpec((part, 256, 128), lambda s, p: (s, 0, 0)),
                pl.BlockSpec((part, 32, 256), lambda s, p: (s, 0, 0)),
                pl.BlockSpec((64, 256), lambda s, p: (0, 0)),
            ],
            out_specs=[
                pl.BlockSpec((32, 48, 128), lambda s, p: (0, 0, 0)),
                pl.BlockSpec((64, 32, 256), lambda s, p: (0, 0, 0)),
            ],
            scratch_shapes=[pltpu.VMEM((32, 32, 256), BF16), pltpu.VMEM((1024, 128), F32)],
        ),
        out_shape=[
            jax.ShapeDtypeStruct((32, 48, 128), BF16),
            jax.ShapeDtypeStruct((64, 32, 256), BF16),
        ],
        compiler_params=pltpu.CompilerParams(vmem_limit_bytes=16 * MB),
        name="reduce_blocks",
    )(places, inverse, rhs, weights, listed)


def choose_kernel(place_ref, received_ref, links_ref, kept_ref, sent_ref, wide, staged):
    for t in range(32):
        wide[t * 16 : t * 16 + 16, :] = received_ref[t, 0:16, :].astype(F32)
    for n in range(32):
        at = pl.multiple_of(place_ref[n] * 8, 8)
        staged[n * 8 : n * 8 + 8, :] = wide[pl.ds(at, 8), :]
    for j in range(8):
        links_ref[j] = staged[pl.ds(j, 32, stride=8), :].astype(BF16)
    for block in range(8):
        rows = [received_ref[block * 4 + s, 16:48, :].astype(F32) for s in range(4)]
        turned = jnp.concatenate(rows, axis=0).T
        lanes = slice(block * 128, block * 128 + 128)
        kept_ref[:, lanes] = turned[:64].astype(BF16)
        sent_ref[:, lanes] = turned[64:].astype(BF16)


def choose_links(places, received):
    return pl.pallas_call(
        choose_kernel,
        in_specs=[
            pl.BlockSpec(memory_space=pltpu.SMEM),
            pl.BlockSpec(memory_space=pltpu.VMEM),
        ],
        out_specs=[pl.BlockSpec(memory_space=pltpu.VMEM)] * 3,
        scratch_shapes=[pltpu.VMEM((512, 128), F32), pltpu.VMEM((256, 128), F32)],
        out_shape=[jax.ShapeDtypeStruct((8, 32, 128), BF16)]
        + [jax.ShapeDtypeStruct((64, 1024), BF16)] * 2,
        compiler_params=pltpu.CompilerParams(vmem_limit_bytes=4 * MB),
        name="choose_links",
    )(places, received)


def turn_kernel(x_ref, a_ref, b_ref, c_ref, d_ref, out_ref, staged):
    for distance, ref in enumerate((a_ref, b_ref, c_ref, d_ref)):
        at = pl.multiple_of((x_ref[0] + distance) % 4 * 32, 32)
        for j in range(8):
            staged[j, pl.ds(at, 32), :] = ref[j].astype(F32)
    for j in range(8):
        out_ref[j * 128 : j * 128 + 128, :] = staged[j].T.astype(BF16)


def turn_links(own_x, blocks):
    return pl.pallas_call(
        turn_kernel,
        in_specs=[pl.BlockSpec(memory_space=pltpu.SMEM)]
        + [pl.BlockSpec(memory_space=pltpu.VMEM)] * 4,
        out_specs=pl.BlockSpec(memory_space=pltpu.VMEM),
        scratch_shapes=[pltpu.VMEM((8, 128, 128), F32)],
        out_shape=jax.ShapeDtypeStruct((1024, 128), BF16),
        compiler_params=pltpu.CompilerParams(vmem_limit_bytes=4 * MB),
        name="turn_links",
    )(own_x, *blocks)


def turn_columns_kernel(kept_ref, came_ref, out_ref):
    for block in range(8):
        lanes = slice(block * 128, block * 128 + 128)
        columns = jnp.concatenate([kept_ref[:, lanes], came_ref[:, lanes]], axis=0)
        out_ref[lanes, :] = columns.astype(F32).T.astype(BF16)


def turn_columns(kept, came):
    return pl.pallas_call(
        turn_columns_kernel,
        in_specs=[pl.BlockSpec(memory_space=pltpu.VMEM)] * 2,
        out_specs=pl.BlockSpec(memory_space=pltpu.VMEM),
        out_shape=jax.ShapeDtypeStruct((1024, 128), BF16),
        compiler_params=pltpu.CompilerParams(vmem_limit_bytes=4 * MB),
        name="turn_columns",
    )(kept, came)


def column_of(j8, j4):
    return j4 * 8 + j8


def collect_kernel(place_ref, names_ref, *rest):
    own, other, (links_ref, parents_ref, sems) = rest[:8], rest[8:16], rest[16:]

    def copies(first, second):
        return [
            pltpu.make_async_copy(refs[d], links_ref.at[which, d], sems.at[which, d])
            for which, refs in enumerate((first, second))
            for d in range(8)
        ]

    def start(first, second):
        for copy in copies(first, second):
            copy.start()

    pl.when(place_ref[0] == 0)(lambda: start(own, other))
    pl.when(place_ref[0] == 1)(lambda: start(other, own))
    lane = lax.broadcasted_iota(jnp.int32, (128, 1024), 1)
    for which in range(2):
        for block in range(8):
            column = names_ref[which : which + 1, block * 128 : block * 128 + 128].T
            parents_ref[which, block * 128 : block * 128 + 128, :] = jnp.where(
                lane == column, 1.0, 0.0
            ).astype(BF16)
    for copy in copies(own, other):
        copy.wait()


def collect(core, names, own, other):
    return pl.pallas_call(
        collect_kernel,
        in_specs=[
            pl.BlockSpec(memory_space=pltpu.SMEM),
            pl.BlockSpec(memory_space=pltpu.VMEM),
        ]
        + [pl.BlockSpec(memory_space=pl.ANY)] * 16,
        out_specs=[pl.BlockSpec(memory_space=pltpu.VMEM)] * 2,
        out_shape=[pltpu.VMEM((2, 8, 1024, 128), BF16), pltpu.VMEM((2, 1024, 1024), BF16)],
        scratch_shapes=[pltpu.SemaphoreType.DMA((2, 8))],
        compiler_params=pltpu.CompilerParams(vmem_limit_bytes=4 * MB),
        name="collect",
    )(core, names, *own, *other)


def multiply_links(lane0, links_ref, source, target):
    lanes = pl.ds(lane0, 128)
    totals = [jnp.zeros((32, 128), F32)] * 2
    for j8 in range(8):
        for j4 in range(4):
            at = (j8 * 4 + j4) * 32
            link = links_ref[at : at + 32, :].astype(F32)
            for c in range(2):
                row = source[pl.ds(c * 32 + column_of(j8, j4), 1), lanes]
                totals[c] = totals[c] + link * row
    for c in range(2):
        target[c * 32 : c * 32 + 32, lanes] = totals[c]


def multiply_links_turned(lane0, links_ref, source, target):
    lanes = pl.ds(lane0, 128)
    columns = [source[c * 32 : c * 32 + 32, lanes] for c in range(2)]
    for j8 in range(8):
        for j4 in range(4):
            at = (j8 * 4 + j4) * 32
            link = links_ref[at : at + 32, :].astype(F32)
            for c in range(2):
                row = jnp.sum(link * columns[c], axis=0, keepdims=True)
                target[pl.ds(c * 32 + column_of(j8, j4), 1), lanes] = row


def by_level(place_ref, kept_ref, came_ref):
    kept, came = kept_ref[...].astype(F32), came_ref[...].astype(F32)
    first = place_ref[1] == 0
    return jnp.where(first, kept, came), jnp.where(first, came, kept)


def gather_parents(names_ref, which, state):
    state = state.astype(F32)
    blocks = [state[:, s * 128 : s * 128 + 128] for s in range(8)]
    chosen = []
    for block in range(8):
        names = names_ref[which : which + 1, block * 128 : block * 128 + 128]
        lane = jnp.broadcast_to(names % 128, (64, 128))
        tile = jnp.broadcast_to(names // 128, (64, 128))
        total = jnp.zeros((64, 128), F32)
        for s in range(8):
            found = jnp.take_along_axis(blocks[s], lane, axis=1, mode="promise_in_bounds")
            total = jnp.where(tile == s, found, total)
        chosen.append(total)
    return jnp.concatenate(chosen, axis=1)


def share(place_ref, first, second, kept_ref, sent_ref):
    kept_ref[...] = jnp.where(place_ref[1] == 0, first, second)
    sent_ref[...] = jnp.where(place_ref[1] == 0, second, first)


def each_block(place_ref, links_ref, which, multiply, source, target):
    for d in range(8):
        lane0 = pl.multiple_of((place_ref[0] + d) % 8 * 128, 128)
        multiply(lane0, links_ref.at[which, d], source, target)


def down_kernel(
    step,
    place_ref,
    kept_ref,
    came_ref,
    own_ref,
    other_ref,
    links_ref,
    parents_ref,
    state_ref,
    next_ref,
    kept_out_ref,
    sent_out_ref,
    source,
    target,
):
    state = jnp.where(place_ref[2] == step, came_ref[...], kept_ref[...])
    state_ref[...] = state
    source[...] = state.astype(F32)
    each_block(place_ref, links_ref, 0, multiply_links, source, target)
    even, odd = by_level(place_ref, own_ref, other_ref)
    low = even - dot(target[...].astype(BF16), parents_ref[0])
    low = low.astype(BF16)
    share(place_ref, state, low, kept_out_ref, sent_out_ref)
    source[...] = low.astype(F32)
    each_block(place_ref, links_ref, 1, multiply_links, source, target)
    high = odd - dot(target[...].astype(BF16), parents_ref[1])
    next_ref[...] = high.astype(BF16)


def up_kernel(
    step,
    place_ref,
    kept_ref,
    came_ref,
    own_ref,
    other_ref,
    links_ref,
    parents_ref,
    state_ref,
    next_ref,
    kept_out_ref,
    sent_out_ref,
    source,
    target,
):
    state = jnp.where(place_ref[2] == step, came_ref[...], kept_ref[...])
    state_ref[...] = state
    source[...] = gather_parents(parents_ref, 1, state)
    each_block(place_ref, links_ref, 1, multiply_links_turned, source, target)
    even, odd = by_level(place_ref, own_ref, other_ref)
    high = (odd - target[...]).astype(BF16)
    share(place_ref, high, state, kept_out_ref, sent_out_ref)
    source[...] = gather_parents(parents_ref, 0, high)
    each_block(place_ref, links_ref, 0, multiply_links_turned, source, target)
    next_ref[...] = (even - target[...]).astype(BF16)


def chain_step(kernel, name, step, place, kept, came, low, high, links, parents):
    links = pltpu.with_memory_space_constraint(links, pltpu.VMEM)
    return pl.pallas_call(
        functools.partial(kernel, step),
        in_specs=[pl.BlockSpec(memory_space=pltpu.SMEM)]
        + [pl.BlockSpec(memory_space=pltpu.VMEM)] * 6,
        out_specs=[pl.BlockSpec(memory_space=pltpu.VMEM)] * 4,
        scratch_shapes=[pltpu.VMEM((64, 1024), F32)] * 2,
        out_shape=[jax.ShapeDtypeStruct((64, 1024), BF16)] * 4,
        compiler_params=pltpu.CompilerParams(vmem_limit_bytes=8 * MB),
        name=name,
    )(place, kept, came, low, high, links, parents)


def middle_kernel(
    place_ref,
    y_ref,
    inverse_ref,
    rhs_ref,
    picks_ref,
    listed_ref,
    forward_ref,
    d_ref,
    wide,
    added,
    solved,
    staged,
    names,
):
    step = pl.program_id(0)
    count = inverse_ref.shape[0]

    @pl.when(step == 0)
    def _():
        added[...] = jnp.zeros_like(added)
        for slot in range(64):
            row = listed_ref[slot : slot + 1, 0:128].astype(jnp.int32)
            names[slot] = jnp.broadcast_to(row, (8, 128))
        for q in range(32):
            wide[q * 64 : q * 64 + 64, :] = y_ref[q].astype(F32)

        def add(slot, carry):
            block = spread(wide[pl.ds(slot, 32, stride=64), :])
            place = place_ref[slot]
            added[place] = added[place] + dot(block, four(picks_ref[slot]))
            return carry

        lax.fori_loop(0, 64, add, 0, unroll=16)

    for k in range(count):
        n = step * count + k
        shifted = (first_half(place_ref, rhs_ref[k].T).astype(F32) - added[n]).astype(BF16)
        forward = dot(shifted, inverse_ref[k], NT).astype(BF16)
        forward_ref[k] = forward
        solved[n] = dot(forward, inverse_ref[k])

    @pl.when(step == pl.num_programs(0) - 1)
    def _():
        def pick(slot, carry):
            named = jnp.concatenate([names[slot]] * 16, axis=0)
            rows = solved[place_ref[slot]]
            halves = [
                jnp.take_along_axis(
                    rows[:, h * 128 : h * 128 + 128], named % 128, axis=1, mode="promise_in_bounds"
                )
                for h in range(2)
            ]
            block = fold(jnp.where(named < 128, halves[0], halves[1]))
            staged[pl.ds(pl.multiple_of(slot * 32, 32), 32), :] = block
            return carry

        lax.fori_loop(0, 64, pick, 0, unroll=16)
        for q in range(32):
            d_ref[q] = staged[pl.ds(q, 64, stride=32), :].astype(BF16)


def middle(places, y_items, inverse, rhs, picks, listed):
    part = 8
    return pl.pallas_call(
        middle_kernel,
        grid_spec=pltpu.PrefetchScalarGridSpec(
            num_scalar_prefetch=1,
            grid=(32 // part,),
            in_specs=[
                pl.BlockSpec((32, 64, 128), lambda s, p: (0, 0, 0)),
                pl.BlockSpec((part, 256, 256), lambda s, p: (s, 0, 0)),
                pl.BlockSpec((part, 256, 128), lambda s, p: (s, 0, 0)),
                pl.BlockSpec((64, 32, 256), lambda s, p: (0, 0, 0)),
                pl.BlockSpec((64, 256), lambda s, p: (0, 0)),
            ],
            out_specs=[
                pl.BlockSpec((part, 128, 256), lambda s, p: (s, 0, 0)),
                pl.BlockSpec((32, 64, 128), lambda s, p: (0, 0, 0)),
            ],
            scratch_shapes=[
                pltpu.VMEM((2048, 128), F32),
                pltpu.VMEM((32, 128, 256), F32),
                pltpu.VMEM((32, 128, 256), F32),
                pltpu.VMEM((2048, 128), F32),
                pltpu.VMEM((64, 8, 128), jnp.int32),
            ],
        ),
        out_shape=[
            jax.ShapeDtypeStruct((32, 128, 256), BF16),
            jax.ShapeDtypeStruct((32, 64, 128), BF16),
        ],
        compiler_params=pltpu.CompilerParams(vmem_limit_bytes=28 * MB),
        name="middle",
    )(places, y_items, inverse, rhs, picks, listed)


def finish_kernel(place_ref, z_ref, forward_ref, inverse_ref, weights_ref, out_ref, wide):
    step = pl.program_id(0)
    count = inverse_ref.shape[0]

    @pl.when(step == 0)
    def _():
        for q in range(32):
            wide[q * 32 : q * 32 + 32, :] = z_ref[q].astype(F32)

    for k in range(count):
        n = step * count + k
        block = spread(wide[pl.ds(n, 32, stride=32), :])
        lowered = forward_ref[k].astype(F32) - dot(block, four(weights_ref[k]))
        solved = dot(lowered.astype(BF16), inverse_ref[k])
        out_ref[k] = first_half(place_ref, solved).T.astype(BF16)


def finish(places, z_items, forward, inverse, weights):
    part = 8
    return pl.pallas_call(
        finish_kernel,
        grid=(32 // part,),
        in_specs=[
            pl.BlockSpec(memory_space=pltpu.SMEM),
            pl.BlockSpec((32, 32, 128), lambda s: (0, 0, 0)),
            pl.BlockSpec((part, 128, 256), lambda s: (s, 0, 0)),
            pl.BlockSpec((part, 256, 256), lambda s: (s, 0, 0)),
            pl.BlockSpec((part, 32, 256), lambda s: (s, 0, 0)),
        ],
        out_specs=pl.BlockSpec((part, 256, 128), lambda s: (s, 0, 0)),
        scratch_shapes=[pltpu.VMEM((1024, 128), F32)],
        out_shape=jax.ShapeDtypeStruct((32, 256, 128), BF16),
        compiler_params=pltpu.CompilerParams(vmem_limit_bytes=16 * MB),
        name="finish",
    )(places, z_items, forward, inverse, weights)


def ring(value, axis, distance):
    size = lax.axis_size(axis)
    return lax.ppermute(value, axis, [(i, (i + distance) % size) for i in range(size)])


def swap(value):
    return lax.ppermute(value, "core", [(0, 1), (1, 0)])


def hop(value, low):
    a, b = (low + 2) % 4, (low + 3) % 4
    return lax.ppermute(value, "y", [(low, low + 1), (low + 1, low), (a, b), (b, a)])


def across(value):
    return lax.all_to_all(value, ("z", "x"), split_axis=0, concat_axis=0, tiled=True)


def gather_links(block):
    ahead, behind = [block], [block]
    for _ in range(3):
        ahead.append(ring(ahead[-1], "z", -1))
        behind.append(ring(behind[-1], "z", 1))
    far = ring(ahead[3], "z", -1)
    return [ahead[0], ahead[1], ahead[2], ahead[3], far, behind[3], behind[2], behind[1]]


def ranks_of(owners):
    by_sub = owners.reshape(32, 32)
    before = jnp.arange(32)[None, :] < jnp.arange(32)[:, None]
    same = (by_sub[:, :, None] == by_sub[:, None, :]) & before[None]
    return jnp.sum(same.astype(jnp.int32), axis=2).reshape(1024)


def on_device(rhs, inverse_blocks, update_blocks, parent_owner, parent_slot, update_rows):
    rhs, inverse, weights = rhs[0], inverse_blocks[0], update_blocks[0]
    z, x = lax.axis_index("z"), lax.axis_index("x")
    plane, core = lax.axis_index("y"), lax.axis_index("core")
    sub, level = z * 4 + x, plane * 2 + core

    def level_of(table, g):
        return lax.dynamic_index_in_dim(table, g, 0, keepdims=False)

    below = jnp.maximum(level - 1, 0)
    owners, slots = level_of(parent_owner[:, :, 0], below), level_of(parent_slot, below)
    rows = level_of(update_rows, below)
    ranks = ranks_of(owners)
    entry = jnp.arange(1024) // 32 * 2 + ranks
    is_child = (owners == sub) & (level > 0)
    hot = jnp.where(is_child[None, :] & (jnp.arange(64)[:, None] == entry[None, :]), 1.0, 0.0)
    listed = jnp.concatenate([rows, rows, rows, rows, slots[:, None], jnp.ones((1024, 1), jnp.int32)], axis=1)
    listed = dot(hot.astype(BF16), jnp.pad(listed, ((0, 0), (0, 126))).astype(BF16))
    places = jnp.concatenate([listed[:, 128].astype(jnp.int32), core[None]])

    items, picks = reduce_blocks(places, inverse, rhs, weights, listed)
    received = across(items)
    own_entry = lax.dynamic_slice_in_dim(owners * 2 + ranks, sub * 32, 32)
    links, c_own, c_sent = choose_links(own_entry, received)
    c_other = swap(c_sent)
    links = turn_links(x[None], [links, ring(links, "x", -1), ring(links, "x", 2), ring(links, "x", 1)])
    own_links = gather_links(links)
    other_links = [swap(block) for block in own_links]

    def parents_of(g):
        return level_of(parent_owner[:, :, 0], g) * 32 + level_of(parent_slot, g)

    names = jnp.stack([parents_of(jnp.maximum(plane * 2 - 1, 0)), parents_of(plane * 2)])
    links, parents = collect(core[None], names, own_links, other_links)
    packing = (
        (owners * 64 + entry)[None, :] == jnp.arange(2048)[:, None]
    ).astype(BF16)

    place = jnp.stack([z, core, plane])
    zeros = jnp.zeros((64, 1024), BF16)
    held = pltpu.with_memory_space_constraint(parents, pltpu.VMEM)
    y_in = came = zeros
    for step in range(4):
        y_in, leaving, kept, sent = chain_step(
            down_kernel, "down", step, place, y_in, came, c_own, c_other, links, held
        )
        if step < 3:
            came = hop(leaving, step)

    y_own = jnp.concatenate([kept, swap(sent)], axis=0)
    y_items = dot(packing, y_own, NT).astype(BF16)
    y_items = across(y_items.reshape(32, 64, 128))
    forward, d_items = middle(places, y_items, inverse, rhs, picks, listed)
    d_items = across(d_items).reshape(2048, 128)
    d_own = lax.dot_general(
        d_items, packing, (((0,), (0,)), ((), ())), preferred_element_type=F32
    ).astype(BF16)
    d_own, d_other = d_own[:64], swap(d_own[64:])

    z_in = came = zeros
    for step in reversed(range(4)):
        z_in, leaving, kept, sent = chain_step(
            up_kernel, "up", step, place, z_in, came, d_own, d_other, links, names
        )
        if step > 0:
            came = hop(leaving, step - 1)

    z_items = across(turn_columns(kept, swap(sent)).reshape(32, 32, 128))
    return finish(places, z_items, forward, inverse, weights)[None]


def solution(mesh):
    fine = Mesh(mesh.devices.reshape(8, 4, 4, 2), ("z", "x", "y", "core"))
    placed = P(("y", "core"), ("z", "x"), None, None)
    return jax.shard_map(
        on_device,
        mesh=fine,
        in_specs=(placed, placed, placed, P(), P(), P()),
        out_specs=placed,
        check_vma=False,
    )
```

```python
import functools
import jax
import jax.numpy as jnp
from jax import lax
from jax.experimental import pallas as pl
from jax.experimental.pallas import tpu as pltpu
from jax.sharding import Mesh
from jax.sharding import PartitionSpec as P

F32 = jnp.float32
BF16 = jnp.bfloat16
NN = (((1,), (0,)), ((), ()))
NT = (((1,), (1,)), ((), ()))
MB = 1 << 20


def dot(a, b, dims=NN):
    return lax.dot_general(a, b, dims, preferred_element_type=F32)


def four(block):
    return jnp.concatenate([block] * 4, axis=0)


def diagonal():
    rows = lax.broadcasted_iota(jnp.int32, (128, 128), 0)
    lanes = lax.broadcasted_iota(jnp.int32, (128, 128), 1)
    return rows // 32 == lanes // 32


def fold(square):
    kept = jnp.where(diagonal(), square, 0.0)
    return kept[:32] + kept[32:64] + kept[64:96] + kept[96:]


def spread(flat):
    return four(flat.astype(BF16)) * jnp.where(diagonal(), 1.0, 0.0).astype(BF16)


PARTS = 8


def part_copies(pairs, sems):
    def copies(part):
        rows = pl.ds(pl.multiple_of(part * (32 // PARTS), 32 // PARTS), 32 // PARTS)
        return [
            pltpu.make_async_copy(source.at[rows], target.at[rows], sems.at[k, part])
            for k, (source, target) in enumerate(pairs)
        ]

    return copies


def first_half(place_ref, block):
    other = jnp.concatenate([block[64:], block[:64]], axis=0)
    return jnp.where(place_ref[64] == 0, block, other)


def reduce_kernel(
    place_ref,
    inverse_hbm,
    rhs_hbm,
    weights_hbm,
    listed_ref,
    out_ref,
    picks_ref,
    inverse,
    rhs,
    weights,
    reduced,
    staged,
    sems,
):
    copies = part_copies(((weights_hbm, weights), (inverse_hbm, inverse), (rhs_hbm, rhs)), sems)
    for part in range(PARTS):
        for copy in copies(part):
            copy.start()
    named = listed_ref[:, 0:128].T[:32]
    filled = listed_ref[:, 128:256].T[1:2]
    named = jnp.where(filled > 0.5, named, -1.0).astype(jnp.int32)
    lane = lax.broadcasted_iota(jnp.int32, (32, 256), 1)
    for slot in range(64):
        hit = jnp.broadcast_to(named[:, slot : slot + 1], (32, 256)) == lane
        picks_ref[slot] = jnp.where(hit, 1.0, 0.0).astype(BF16)

    def reduce_part(part, carry):
        for copy in copies(part):
            copy.wait()
        for k in range(32 // PARTS):
            n = part * (32 // PARTS) + k
            product = dot(weights[n], inverse[n]).astype(BF16)
            reduced[n] = product
            columns = fold(dot(first_half(place_ref, rhs[n].T), four(product), NT))
            staged[pl.ds(pl.multiple_of(n * 32, 32), 32), :] = columns
        return carry

    lax.fori_loop(0, PARTS, reduce_part, 0, unroll=2)
    for q in range(32):
        out_ref[q, 16:48, :] = staged[pl.ds(q, 32, stride=32), :].astype(BF16)
    group = lax.broadcasted_iota(jnp.int32, (8, 128), 1) // 32

    def link(pair, carry):
        halves = []
        for r in range(2):
            slot = pair * 2 + r
            wide = dot(picks_ref[slot], four(reduced[place_ref[slot]]), NT)
            parts = [jnp.where(group == j, wide[j * 8 : j * 8 + 8], 0.0) for j in range(4)]
            halves.append(parts[0] + parts[1] + parts[2] + parts[3])
        out_ref[pair, 0:16, :] = jnp.concatenate(halves, axis=0).astype(BF16)
        return carry

    lax.fori_loop(0, 32, link, 0, unroll=16)


def reduce_blocks(places, inverse, rhs, weights, listed):
    return pl.pallas_call(
        reduce_kernel,
        in_specs=[pl.BlockSpec(memory_space=pltpu.SMEM)]
        + [pl.BlockSpec(memory_space=pltpu.HBM)] * 3
        + [pl.BlockSpec(memory_space=pltpu.VMEM)],
        out_specs=[pl.BlockSpec(memory_space=pltpu.VMEM)] * 2,
        scratch_shapes=[
            pltpu.VMEM((32, 256, 256), BF16),
            pltpu.VMEM((32, 256, 128), BF16),
            pltpu.VMEM((32, 32, 256), BF16),
            pltpu.VMEM((32, 32, 256), BF16),
            pltpu.VMEM((1024, 128), F32),
            pltpu.SemaphoreType.DMA((3, PARTS)),
        ],
        out_shape=[
            jax.ShapeDtypeStruct((32, 48, 128), BF16),
            jax.ShapeDtypeStruct((64, 32, 256), BF16),
        ],
        compiler_params=pltpu.CompilerParams(vmem_limit_bytes=58 * MB),
        name="reduce_blocks",
    )(places, inverse, rhs, weights, listed)


def choose_kernel(place_ref, received_ref, links_ref, kept_ref, sent_ref, wide, staged):
    for t in range(32):
        wide[t * 16 : t * 16 + 16, :] = received_ref[t, 0:16, :].astype(F32)
    for n in range(32):
        at = pl.multiple_of(place_ref[n] * 8, 8)
        staged[n * 8 : n * 8 + 8, :] = wide[pl.ds(at, 8), :]
    for j in range(8):
        links_ref[j] = staged[pl.ds(j, 32, stride=8), :].astype(BF16)
    for block in range(8):
        rows = [received_ref[block * 4 + s, 16:48, :].astype(F32) for s in range(4)]
        turned = jnp.concatenate(rows, axis=0).T
        lanes = slice(block * 128, block * 128 + 128)
        kept_ref[:, lanes] = turned[:64].astype(BF16)
        sent_ref[:, lanes] = turned[64:].astype(BF16)


def choose_links(places, received):
    return pl.pallas_call(
        choose_kernel,
        in_specs=[
            pl.BlockSpec(memory_space=pltpu.SMEM),
            pl.BlockSpec(memory_space=pltpu.VMEM),
        ],
        out_specs=[pl.BlockSpec(memory_space=pltpu.VMEM)] * 3,
        scratch_shapes=[pltpu.VMEM((512, 128), F32), pltpu.VMEM((256, 128), F32)],
        out_shape=[jax.ShapeDtypeStruct((8, 32, 128), BF16)]
        + [jax.ShapeDtypeStruct((64, 1024), BF16)] * 2,
        compiler_params=pltpu.CompilerParams(vmem_limit_bytes=4 * MB),
        name="choose_links",
    )(places, received)


def turn_kernel(x_ref, a_ref, b_ref, c_ref, d_ref, out_ref, staged):
    for distance, ref in enumerate((a_ref, b_ref, c_ref, d_ref)):
        at = pl.multiple_of((x_ref[0] + distance) % 4 * 32, 32)
        for j in range(8):
            staged[j, pl.ds(at, 32), :] = ref[j].astype(F32)
    for j in range(8):
        out_ref[j * 128 : j * 128 + 128, :] = staged[j].T.astype(BF16)


def turn_links(own_x, blocks):
    return pl.pallas_call(
        turn_kernel,
        in_specs=[pl.BlockSpec(memory_space=pltpu.SMEM)]
        + [pl.BlockSpec(memory_space=pltpu.VMEM)] * 4,
        out_specs=pl.BlockSpec(memory_space=pltpu.VMEM),
        scratch_shapes=[pltpu.VMEM((8, 128, 128), F32)],
        out_shape=jax.ShapeDtypeStruct((1024, 128), BF16),
        compiler_params=pltpu.CompilerParams(vmem_limit_bytes=4 * MB),
        name="turn_links",
    )(own_x, *blocks)


def turn_columns_kernel(kept_ref, came_ref, out_ref):
    for block in range(8):
        lanes = slice(block * 128, block * 128 + 128)
        columns = jnp.concatenate([kept_ref[:, lanes], came_ref[:, lanes]], axis=0)
        out_ref[lanes, :] = columns.astype(F32).T.astype(BF16)


def turn_columns(kept, came):
    return pl.pallas_call(
        turn_columns_kernel,
        in_specs=[pl.BlockSpec(memory_space=pltpu.VMEM)] * 2,
        out_specs=pl.BlockSpec(memory_space=pltpu.VMEM),
        out_shape=jax.ShapeDtypeStruct((1024, 128), BF16),
        compiler_params=pltpu.CompilerParams(vmem_limit_bytes=4 * MB),
        name="turn_columns",
    )(kept, came)


def column_of(j8, j4):
    return j4 * 8 + j8


def collect_kernel(place_ref, names_ref, *rest):
    own, other, (links_ref, parents_ref, sems) = rest[:8], rest[8:16], rest[16:]

    def copies(first, second):
        return [
            pltpu.make_async_copy(refs[d], links_ref.at[which, d], sems.at[which, d])
            for which, refs in enumerate((first, second))
            for d in range(8)
        ]

    def start(first, second):
        for copy in copies(first, second):
            copy.start()

    pl.when(place_ref[0] == 0)(lambda: start(own, other))
    pl.when(place_ref[0] == 1)(lambda: start(other, own))
    lane = lax.broadcasted_iota(jnp.int32, (128, 1024), 1)
    for which in range(2):
        for block in range(8):
            column = names_ref[which : which + 1, block * 128 : block * 128 + 128].T
            parents_ref[which, block * 128 : block * 128 + 128, :] = jnp.where(
                lane == column, 1.0, 0.0
            ).astype(BF16)
    for copy in copies(own, other):
        copy.wait()


def collect(core, names, own, other):
    return pl.pallas_call(
        collect_kernel,
        in_specs=[
            pl.BlockSpec(memory_space=pltpu.SMEM),
            pl.BlockSpec(memory_space=pltpu.VMEM),
        ]
        + [pl.BlockSpec(memory_space=pl.ANY)] * 16,
        out_specs=[pl.BlockSpec(memory_space=pltpu.VMEM)] * 2,
        out_shape=[pltpu.VMEM((2, 8, 1024, 128), BF16), pltpu.VMEM((2, 1024, 1024), BF16)],
        scratch_shapes=[pltpu.SemaphoreType.DMA((2, 8))],
        compiler_params=pltpu.CompilerParams(vmem_limit_bytes=4 * MB),
        name="collect",
    )(core, names, *own, *other)


def multiply_links(lane0, links_ref, source, target):
    lanes = pl.ds(lane0, 128)
    totals = [jnp.zeros((32, 128), F32)] * 2
    for j8 in range(8):
        for j4 in range(4):
            at = (j8 * 4 + j4) * 32
            link = links_ref[at : at + 32, :].astype(F32)
            for c in range(2):
                row = source[pl.ds(c * 32 + column_of(j8, j4), 1), lanes]
                totals[c] = totals[c] + link * row
    for c in range(2):
        target[c * 32 : c * 32 + 32, lanes] = totals[c]


def multiply_links_turned(lane0, links_ref, source, target):
    lanes = pl.ds(lane0, 128)
    columns = [source[c * 32 : c * 32 + 32, lanes] for c in range(2)]
    for j8 in range(8):
        for j4 in range(4):
            at = (j8 * 4 + j4) * 32
            link = links_ref[at : at + 32, :].astype(F32)
            for c in range(2):
                row = jnp.sum(link * columns[c], axis=0, keepdims=True)
                target[pl.ds(c * 32 + column_of(j8, j4), 1), lanes] = row


def by_level(place_ref, kept_ref, came_ref):
    kept, came = kept_ref[...].astype(F32), came_ref[...].astype(F32)
    first = place_ref[1] == 0
    return jnp.where(first, kept, came), jnp.where(first, came, kept)


def gather_parents(names_ref, which, state):
    state = state.astype(F32)
    blocks = [state[:, s * 128 : s * 128 + 128] for s in range(8)]
    chosen = []
    for block in range(8):
        names = names_ref[which : which + 1, block * 128 : block * 128 + 128]
        lane = jnp.broadcast_to(names % 128, (64, 128))
        tile = jnp.broadcast_to(names // 128, (64, 128))
        total = jnp.zeros((64, 128), F32)
        for s in range(8):
            found = jnp.take_along_axis(blocks[s], lane, axis=1, mode="promise_in_bounds")
            total = jnp.where(tile == s, found, total)
        chosen.append(total)
    return jnp.concatenate(chosen, axis=1)


def share(place_ref, first, second, kept_ref, sent_ref):
    kept_ref[...] = jnp.where(place_ref[1] == 0, first, second)
    sent_ref[...] = jnp.where(place_ref[1] == 0, second, first)


def each_block(place_ref, links_ref, which, multiply, source, target):
    for d in range(8):
        lane0 = pl.multiple_of((place_ref[0] + d) % 8 * 128, 128)
        multiply(lane0, links_ref.at[which, d], source, target)


def down_kernel(
    step,
    place_ref,
    kept_ref,
    came_ref,
    own_ref,
    other_ref,
    links_ref,
    parents_ref,
    state_ref,
    next_ref,
    kept_out_ref,
    sent_out_ref,
    source,
    target,
):
    state = jnp.where(place_ref[2] == step, came_ref[...], kept_ref[...])
    state_ref[...] = state
    source[...] = state.astype(F32)
    each_block(place_ref, links_ref, 0, multiply_links, source, target)
    even, odd = by_level(place_ref, own_ref, other_ref)
    low = even - dot(target[...].astype(BF16), parents_ref[0])
    low = low.astype(BF16)
    share(place_ref, state, low, kept_out_ref, sent_out_ref)
    source[...] = low.astype(F32)
    each_block(place_ref, links_ref, 1, multiply_links, source, target)
    high = odd - dot(target[...].astype(BF16), parents_ref[1])
    next_ref[...] = high.astype(BF16)


def up_kernel(
    step,
    place_ref,
    kept_ref,
    came_ref,
    own_ref,
    other_ref,
    links_ref,
    parents_ref,
    state_ref,
    next_ref,
    kept_out_ref,
    sent_out_ref,
    source,
    target,
):
    state = jnp.where(place_ref[2] == step, came_ref[...], kept_ref[...])
    state_ref[...] = state
    source[...] = gather_parents(parents_ref, 1, state)
    each_block(place_ref, links_ref, 1, multiply_links_turned, source, target)
    even, odd = by_level(place_ref, own_ref, other_ref)
    high = (odd - target[...]).astype(BF16)
    share(place_ref, high, state, kept_out_ref, sent_out_ref)
    source[...] = gather_parents(parents_ref, 0, high)
    each_block(place_ref, links_ref, 0, multiply_links_turned, source, target)
    next_ref[...] = (even - target[...]).astype(BF16)


def chain_step(kernel, name, step, place, kept, came, low, high, links, parents):
    links = pltpu.with_memory_space_constraint(links, pltpu.VMEM)
    return pl.pallas_call(
        functools.partial(kernel, step),
        in_specs=[pl.BlockSpec(memory_space=pltpu.SMEM)]
        + [pl.BlockSpec(memory_space=pltpu.VMEM)] * 6,
        out_specs=[pl.BlockSpec(memory_space=pltpu.VMEM)] * 4,
        scratch_shapes=[pltpu.VMEM((64, 1024), F32)] * 2,
        out_shape=[jax.ShapeDtypeStruct((64, 1024), BF16)] * 4,
        compiler_params=pltpu.CompilerParams(vmem_limit_bytes=8 * MB),
        name=name,
    )(place, kept, came, low, high, links, parents)


def middle_kernel(
    place_ref, y_ref, inverse_ref, rhs_ref, picks_ref, forward_ref, d_ref, wide, added, solved, staged
):
    step = pl.program_id(0)
    count = inverse_ref.shape[0]

    @pl.when(step == 0)
    def _():
        added[...] = jnp.zeros_like(added)
        for q in range(32):
            wide[q * 64 : q * 64 + 64, :] = y_ref[q].astype(F32)

        def add(slot, carry):
            block = spread(wide[pl.ds(slot, 32, stride=64), :])
            place = place_ref[slot]
            added[place] = added[place] + dot(block, four(picks_ref[slot]))
            return carry

        lax.fori_loop(0, 64, add, 0, unroll=16)

    for k in range(count):
        n = step * count + k
        shifted = (first_half(place_ref, rhs_ref[k].T).astype(F32) - added[n]).astype(BF16)
        forward = dot(shifted, inverse_ref[k], NT).astype(BF16)
        forward_ref[k] = forward
        solved[n] = dot(forward, inverse_ref[k]).astype(BF16)

    @pl.when(step == pl.num_programs(0) - 1)
    def _():
        def pick(slot, carry):
            block = fold(dot(solved[place_ref[slot]], four(picks_ref[slot]), NT))
            staged[pl.ds(pl.multiple_of(slot * 32, 32), 32), :] = block
            return carry

        lax.fori_loop(0, 64, pick, 0, unroll=16)
        for q in range(32):
            d_ref[q] = staged[pl.ds(q, 64, stride=32), :].astype(BF16)


def middle(places, y_items, inverse, rhs, picks):
    part = 8
    return pl.pallas_call(
        middle_kernel,
        grid_spec=pltpu.PrefetchScalarGridSpec(
            num_scalar_prefetch=1,
            grid=(32 // part,),
            in_specs=[
                pl.BlockSpec((32, 64, 128), lambda s, p: (0, 0, 0)),
                pl.BlockSpec((part, 256, 256), lambda s, p: (s, 0, 0)),
                pl.BlockSpec((part, 256, 128), lambda s, p: (s, 0, 0)),
                pl.BlockSpec((64, 32, 256), lambda s, p: (0, 0, 0)),
            ],
            out_specs=[
                pl.BlockSpec((part, 128, 256), lambda s, p: (s, 0, 0)),
                pl.BlockSpec((32, 64, 128), lambda s, p: (0, 0, 0)),
            ],
            scratch_shapes=[
                pltpu.VMEM((2048, 128), F32),
                pltpu.VMEM((32, 128, 256), F32),
                pltpu.VMEM((32, 128, 256), BF16),
                pltpu.VMEM((2048, 128), F32),
            ],
        ),
        out_shape=[
            jax.ShapeDtypeStruct((32, 128, 256), BF16),
            jax.ShapeDtypeStruct((32, 64, 128), BF16),
        ],
        compiler_params=pltpu.CompilerParams(vmem_limit_bytes=24 * MB),
        name="middle",
    )(places, y_items, inverse, rhs, picks)


def finish_kernel(place_ref, z_ref, forward_ref, inverse_ref, weights_ref, out_ref, wide):
    step = pl.program_id(0)
    count = inverse_ref.shape[0]

    @pl.when(step == 0)
    def _():
        for q in range(32):
            wide[q * 32 : q * 32 + 32, :] = z_ref[q].astype(F32)

    for k in range(count):
        n = step * count + k
        block = spread(wide[pl.ds(n, 32, stride=32), :])
        lowered = forward_ref[k].astype(F32) - dot(block, four(weights_ref[k]))
        solved = dot(lowered.astype(BF16), inverse_ref[k])
        out_ref[k] = first_half(place_ref, solved).T.astype(BF16)


def finish(places, z_items, forward, inverse, weights):
    part = 8
    return pl.pallas_call(
        finish_kernel,
        grid=(32 // part,),
        in_specs=[
            pl.BlockSpec(memory_space=pltpu.SMEM),
            pl.BlockSpec((32, 32, 128), lambda s: (0, 0, 0)),
            pl.BlockSpec((part, 128, 256), lambda s: (s, 0, 0)),
            pl.BlockSpec((part, 256, 256), lambda s: (s, 0, 0)),
            pl.BlockSpec((part, 32, 256), lambda s: (s, 0, 0)),
        ],
        out_specs=pl.BlockSpec((part, 256, 128), lambda s: (s, 0, 0)),
        scratch_shapes=[pltpu.VMEM((1024, 128), F32)],
        out_shape=jax.ShapeDtypeStruct((32, 256, 128), BF16),
        compiler_params=pltpu.CompilerParams(vmem_limit_bytes=16 * MB),
        name="finish",
    )(places, z_items, forward, inverse, weights)


def ring(value, axis, distance):
    size = lax.axis_size(axis)
    return lax.ppermute(value, axis, [(i, (i + distance) % size) for i in range(size)])


def swap(value):
    return lax.ppermute(value, "core", [(0, 1), (1, 0)])


def hop(value, low):
    a, b = (low + 2) % 4, (low + 3) % 4
    return lax.ppermute(value, "y", [(low, low + 1), (low + 1, low), (a, b), (b, a)])


def across(value):
    return lax.all_to_all(value, ("z", "x"), split_axis=0, concat_axis=0, tiled=True)


def gather_links(block):
    ahead, behind = [block], [block]
    for _ in range(3):
        ahead.append(ring(ahead[-1], "z", -1))
        behind.append(ring(behind[-1], "z", 1))
    far = ring(ahead[3], "z", -1)
    return [ahead[0], ahead[1], ahead[2], ahead[3], far, behind[3], behind[2], behind[1]]


def ranks_of(owners):
    by_sub = owners.reshape(32, 32)
    before = jnp.arange(32)[None, :] < jnp.arange(32)[:, None]
    same = (by_sub[:, :, None] == by_sub[:, None, :]) & before[None]
    return jnp.sum(same.astype(jnp.int32), axis=2).reshape(1024)


def on_device(rhs, inverse_blocks, update_blocks, parent_owner, parent_slot, update_rows):
    rhs, inverse, weights = rhs[0], inverse_blocks[0], update_blocks[0]
    z, x = lax.axis_index("z"), lax.axis_index("x")
    plane, core = lax.axis_index("y"), lax.axis_index("core")
    sub, level = z * 4 + x, plane * 2 + core

    def level_of(table, g):
        return lax.dynamic_index_in_dim(table, g, 0, keepdims=False)

    below = jnp.maximum(level - 1, 0)
    owners, slots = level_of(parent_owner[:, :, 0], below), level_of(parent_slot, below)
    rows = level_of(update_rows, below)
    ranks = ranks_of(owners)
    entry = jnp.arange(1024) // 32 * 2 + ranks
    is_child = (owners == sub) & (level > 0)
    hot = jnp.where(is_child[None, :] & (jnp.arange(64)[:, None] == entry[None, :]), 1.0, 0.0)
    listed = jnp.concatenate([rows, rows, rows, rows, slots[:, None], jnp.ones((1024, 1), jnp.int32)], axis=1)
    listed = dot(hot.astype(BF16), jnp.pad(listed, ((0, 0), (0, 126))).astype(BF16))
    places = jnp.concatenate([listed[:, 128].astype(jnp.int32), core[None]])

    items, picks = reduce_blocks(places, inverse, rhs, weights, listed)
    received = across(items)
    own_entry = lax.dynamic_slice_in_dim(owners * 2 + ranks, sub * 32, 32)
    links, c_own, c_sent = choose_links(own_entry, received)
    c_other = swap(c_sent)
    links = turn_links(x[None], [links, ring(links, "x", -1), ring(links, "x", 2), ring(links, "x", 1)])
    own_links = gather_links(links)
    other_links = [swap(block) for block in own_links]

    def parents_of(g):
        return level_of(parent_owner[:, :, 0], g) * 32 + level_of(parent_slot, g)

    names = jnp.stack([parents_of(jnp.maximum(plane * 2 - 1, 0)), parents_of(plane * 2)])
    links, parents = collect(core[None], names, own_links, other_links)
    packing = (
        (owners * 64 + entry)[None, :] == jnp.arange(2048)[:, None]
    ).astype(BF16)

    place = jnp.stack([z, core, plane])
    zeros = jnp.zeros((64, 1024), BF16)
    held = pltpu.with_memory_space_constraint(parents, pltpu.VMEM)
    y_in = came = zeros
    for step in range(4):
        y_in, leaving, kept, sent = chain_step(
            down_kernel, "down", step, place, y_in, came, c_own, c_other, links, held
        )
        if step < 3:
            came = hop(leaving, step)

    y_own = jnp.concatenate([kept, swap(sent)], axis=0)
    y_items = dot(packing, y_own, NT).astype(BF16)
    y_items = across(y_items.reshape(32, 64, 128))
    forward, d_items = middle(places, y_items, inverse, rhs, picks)
    d_items = across(d_items).reshape(2048, 128)
    d_own = lax.dot_general(
        d_items, packing, (((0,), (0,)), ((), ())), preferred_element_type=F32
    ).astype(BF16)
    d_own, d_other = d_own[:64], swap(d_own[64:])

    z_in = came = zeros
    for step in reversed(range(4)):
        z_in, leaving, kept, sent = chain_step(
            up_kernel, "up", step, place, z_in, came, d_own, d_other, links, names
        )
        if step > 0:
            came = hop(leaving, step - 1)

    z_items = across(turn_columns(kept, swap(sent)).reshape(32, 32, 128))
    return finish(places, z_items, forward, inverse, weights)[None]


def solution(mesh):
    fine = Mesh(mesh.devices.reshape(8, 4, 4, 2), ("z", "x", "y", "core"))
    placed = P(("y", "core"), ("z", "x"), None, None)
    return jax.shard_map(
        on_device,
        mesh=fine,
        in_specs=(placed, placed, placed, P(), P(), P()),
        out_specs=placed,
        check_vma=False,
    )
```
